512 devices in a mesh: row: 32 (over z_lo, x), col: 16 (over y, z_hi, core).
Axes of the slice: x: 4, y: 4, z: 16 (z_hi: 2, z_lo: 8; z = z_hi * 8 + z_lo), core: 2. Of those that a mesh axis runs over, the one named last changes fastest.
Arguments:
- tokens: bfloat16 [4096, 6144], P('row', 'col'), may hold values from -6 to 6
- w_up: bfloat16 [2048, 4096], P('row', 'col'), may hold values from -0.3125 to 0.3125
- up_feat: int32 [32, 64], P('row', 'col'), may hold values from 0 to 2, as said below
- up_hid: int32 [32, 64], P('row', 'col'), may hold values from 0 to 23
- up_count: int32 [32, 16], P('row', 'col'), may hold values from 2 to 4, as said below
- w_down: bfloat16 [2048, 4096], P('row', 'col'), may hold values from -0.15625 to 0.15625
- down_feat: int32 [32, 64], P('row', 'col'), may hold values from 0 to 2, as said below
- down_hid: int32 [32, 64], P('row', 'col'), may hold values from 0 to 23
- down_count: int32 [32, 16], P('row', 'col'), may hold values from 2 to 4, as said below
- grad_out: bfloat16 [4096, 6144], P('row', 'col'), may hold values from -1 to 1
Outputs:
- mixed: bfloat16 [4096, 6144], P('row', 'col')
- grad_in: bfloat16 [4096, 6144], P('row', 'col')
- grad_up: bfloat16 [2048, 4096], P('row', 'col')
- grad_down: bfloat16 [2048, 4096], P('row', 'col')
The draws below stay inside these ranges and needn't reach their ends.
Inputs may be any that keep to these rules, and one draw needn't show every extreme that they name: For each tile, the pairs (up_feat, up_hid) of its 4 slots are distinct. `up_count`: slots at or beyond a tile's count are unused; some tile has 4. For each tile, the pairs (down_feat, down_hid) of its 4 slots are distinct. `down_count`: slots at or beyond a tile's count are unused; some tile has 4.
All inputs are finite; a program needn't handle non-finite values.
Results may differ from the reference program's by a relative error of at most 0.015.
Values may be sent and summed in bfloat16 or wider, within the bound.
A program may use at most 64 MiB of HBM per device.

```python
import jax
import jax.numpy as jnp
from jax import lax

D = 6144
H = 24576
BLK = 64
TOK_DEV = 128
TOKENS = 4096
HID_DEV = 1536
FEAT_BLK = 3
HID_BLK = 24
CAP = 4
N_ROW = 32
N_COL = 16


def block_pattern(key, offset_code):
    pattern_key = jax.random.fold_in(key, offset_code)
    tile_total = N_ROW * N_COL
    tile_keys = jax.random.split(jax.random.fold_in(pattern_key, 1), tile_total)
    chosen = jax.vmap(lambda tile_key: jax.random.permutation(tile_key, FEAT_BLK * HID_BLK)[:CAP])(tile_keys)
    chosen = chosen.astype(jnp.int32)
    features = (chosen // HID_BLK).reshape(N_ROW, N_COL * CAP)
    hiddens = (chosen % HID_BLK).reshape(N_ROW, N_COL * CAP)
    counts = jax.random.randint(jax.random.fold_in(pattern_key, 2), (tile_total,), CAP // 2, CAP + 1)
    filled = jax.random.randint(jax.random.fold_in(pattern_key, 3), (), 0, tile_total)
    counts = jnp.where(jnp.arange(tile_total) == filled, CAP, counts)
    return (features.astype(jnp.int32), hiddens.astype(jnp.int32), counts.reshape(N_ROW, N_COL).astype(jnp.int32))


def draw_up_feat(key, part):
    return block_pattern(key, 5)[0]


def draw_up_hid(key, part):
    return block_pattern(key, 5)[1]


def draw_up_count(key, part):
    return block_pattern(key, 5)[2]


def draw_down_feat(key, part):
    return block_pattern(key, 9)[0]


def draw_down_hid(key, part):
    return block_pattern(key, 9)[1]


def draw_down_count(key, part):
    return block_pattern(key, 9)[2]


def levels(rng, extent, cuts, low, top_value):
    def one(dim, blocks):
        steps = jax.random.uniform(jax.random.fold_in(jax.random.fold_in(rng, 6), dim), (blocks,), jnp.float32, low / len(cuts), top_value / len(cuts))
        return jnp.repeat(jnp.exp(steps), extent[dim] // blocks).reshape((-1,) + (1,) * (len(extent) - dim - 1))

    factor_of = one(*cuts[0])
    for cut in cuts[1:]:
        factor_of = factor_of * one(*cut)
    return factor_of


def bell_draw(key, shape, spread, most, cuts=(), held_as=jnp.bfloat16):
    entries = spread * jax.random.normal(key, shape, jnp.float32)
    if cuts:
        entries = entries * levels(key, shape, cuts, -0.22, 0.18)
    return jnp.clip(entries, -most, most).astype(held_as)


def setup_inputs(seed: int = 0) -> dict:
    key_of = jax.random.split(jax.random.key(seed), 11)
    tokens = bell_draw(key_of[0], (TOKENS, D), 1.0, 6.0, ((0, 32), (1, 16)))
    w_up = bell_draw(key_of[1], (N_ROW * BLK, N_COL * CAP * BLK), (BLK * CAP * N_ROW * BLK * N_COL // H) ** -0.5, 0.3125, ((0, 32), (1, 16)))
    up_feat = draw_up_feat(jax.random.fold_in(key_of[10], 71), 0)
    up_hid = draw_up_hid(jax.random.fold_in(key_of[10], 71), 0)
    up_count = draw_up_count(jax.random.fold_in(key_of[10], 71), 0)
    w_down = bell_draw(key_of[5], (N_ROW * BLK, N_COL * CAP * BLK), (BLK * CAP * N_COL * BLK * N_ROW // D) ** -0.5, 0.15625, ((0, 32), (1, 16)))
    down_feat = draw_down_feat(jax.random.fold_in(key_of[10], 71), 0)
    down_hid = draw_down_hid(jax.random.fold_in(key_of[10], 71), 0)
    down_count = draw_down_count(jax.random.fold_in(key_of[10], 71), 0)
    grad_out = bell_draw(key_of[9], (TOKENS, D), 0.125, 1.0, ((0, 32), (1, 16)))
    return dict(tokens=tokens, w_up=w_up, up_feat=up_feat, up_hid=up_hid, up_count=up_count, w_down=w_down, down_feat=down_feat, down_hid=down_hid, down_count=down_count, grad_out=grad_out)


GELU_SCALE = 0.7978845608028654
GELU_CUBIC = 0.044715


def gelu_parts(hidden_pre):
    argument = GELU_SCALE * (hidden_pre + GELU_CUBIC * hidden_pre * hidden_pre * hidden_pre)
    tanh_value = jnp.tanh(argument)
    values = 0.5 * hidden_pre * (1.0 + tanh_value)
    derivative = 0.5 * (1.0 + tanh_value) + 0.5 * hidden_pre * (1.0 - tanh_value * tanh_value) * GELU_SCALE * (1.0 + 3.0 * GELU_CUBIC * hidden_pre * hidden_pre)
    return values, derivative


def rounded(values):
    return lax.optimization_barrier(values.astype(jnp.bfloat16)).astype(jnp.float32)


def column_tiles(block_values, features, hiddens, counts, column):
    first_slot = column * CAP
    shaped = lax.dynamic_slice_in_dim(block_values, first_slot * BLK, CAP * BLK, 1).reshape(N_ROW, BLK, CAP, BLK)
    feature_idx = lax.dynamic_slice_in_dim(features, first_slot, CAP, 1)
    hidden_idx = lax.dynamic_slice_in_dim(hiddens, first_slot, CAP, 1)
    tile_counts = lax.dynamic_slice_in_dim(counts, column, 1, 1)
    is_live = jnp.arange(CAP, dtype=jnp.int32)[None, :] < tile_counts
    return shaped, feature_idx, hidden_idx, is_live


def pick_blocks(source, indices, block_total):
    row_count = source.shape[0]
    blocks = source.reshape(row_count, block_total, BLK)
    return jnp.take(blocks, indices.reshape(-1).astype(jnp.int32), axis=1).reshape(row_count, N_ROW, CAP, BLK)


def block_grads(left_side, right_side):
    left_groups = left_side.astype(jnp.float32).reshape(N_ROW, TOK_DEV, N_ROW, CAP, BLK)
    right_groups = right_side.astype(jnp.float32).reshape(N_ROW, TOK_DEV, N_ROW, CAP, BLK)
    partials = jnp.einsum('gtrsi,gtrsj->grisj', left_groups, right_groups)
    summed = jnp.sum(rounded(partials), axis=0)
    return summed.astype(jnp.bfloat16).reshape(N_ROW * BLK, CAP * BLK)


def reference(tokens, w_up, up_feat, up_hid, up_count, w_down, down_feat, down_hid, down_count, grad_out):
    highest = lax.Precision.HIGHEST
    row_base = jnp.arange(N_ROW, dtype=jnp.int32)[:, None] * FEAT_BLK
    hidden_range = jnp.arange(HID_BLK, dtype=jnp.int32)
    feature_range = jnp.arange(FEAT_BLK, dtype=jnp.int32)

    def column_step(carried, column):
        mixed_sum, grad_sum = carried
        up_values, up_feature, up_hidden, up_live = column_tiles(w_up, up_feat, up_hid, up_count, column)
        down_values, down_feature, down_hidden, down_live = column_tiles(w_down, down_feat, down_hid, down_count, column)
        token_pick = pick_blocks(tokens, row_base + up_feature, D // BLK)
        product = jnp.einsum('trsi,risj->trsj', token_pick.astype(jnp.float32), up_values.astype(jnp.float32))
        up_onehot = ((up_hidden[:, :, None] == hidden_range) & up_live[:, :, None]).astype(jnp.float32)
        hidden_pre = jnp.einsum('trsj,rsk->tkj', product, up_onehot, precision=highest).reshape(TOKENS, HID_DEV)
        values, derivative = gelu_parts(hidden_pre)
        activation = values.astype(jnp.bfloat16)
        active_pick = pick_blocks(activation, down_hidden, HID_BLK)
        product = jnp.einsum('trsi,risj->trsj', active_pick.astype(jnp.float32), down_values.astype(jnp.float32))
        down_onehot = ((down_feature[:, :, None] == feature_range) & down_live[:, :, None]).astype(jnp.float32)
        partial_value = jnp.einsum('trsj,rsf->trfj', product, down_onehot, precision=highest).reshape(TOKENS, D)
        mixed_sum = mixed_sum + rounded(partial_value)
        down_mask = down_live.astype(jnp.bfloat16)[None, :, :, None]
        output_pick = pick_blocks(grad_out, row_base + down_feature, D // BLK) * down_mask
        product = jnp.einsum('trsj,risj->trsi', output_pick.astype(jnp.float32), down_values.astype(jnp.float32))
        down_hot = (down_hidden[:, :, None] == hidden_range).astype(jnp.float32)
        back = jnp.einsum('trsi,rsk->tki', product, down_hot, precision=highest).reshape(TOKENS, HID_DEV)
        grad_pre = (back * derivative).astype(jnp.bfloat16)
        up_mask = up_live.astype(jnp.bfloat16)[None, :, :, None]
        hidden_pick = pick_blocks(grad_pre, up_hidden, HID_BLK) * up_mask
        product = jnp.einsum('trsj,risj->trsi', hidden_pick.astype(jnp.float32), up_values.astype(jnp.float32))
        up_hot = (up_feature[:, :, None] == feature_range).astype(jnp.float32)
        partial_value = jnp.einsum('trsi,rsf->trfi', product, up_hot, precision=highest).reshape(TOKENS, D)
        grad_sum = grad_sum + rounded(partial_value)
        grad_down = block_grads(active_pick, output_pick)
        grad_up = block_grads(token_pick, hidden_pick)
        return (mixed_sum, grad_sum), (grad_up, grad_down)

    start_sums = (jnp.zeros((TOKENS, D), jnp.float32), jnp.zeros((TOKENS, D), jnp.float32))
    sums, stacked = lax.scan(column_step, start_sums, jnp.arange(N_COL, dtype=jnp.int32))
    mixed_sum, grad_sum = sums
    grad_up = stacked[0].transpose(1, 0, 2).reshape(N_ROW * BLK, N_COL * CAP * BLK)
    grad_down = stacked[1].transpose(1, 0, 2).reshape(N_ROW * BLK, N_COL * CAP * BLK)
    return mixed_sum.astype(jnp.bfloat16), grad_sum.astype(jnp.bfloat16), grad_up, grad_down
```

```python
import jax
import jax.numpy as jnp
from jax import lax
from jax.experimental import pallas as pl
from jax.experimental.pallas import tpu as pltpu
from jax.sharding import PartitionSpec as P

BLK = 64
CAP = 4
TOK = 128
FEAT = 384
HB = 24
NX, NY, NZ = 4, 4, 8
UNITS = 16
ROWS = 32
GELU_SCALE = 0.7978845608028654
GELU_CUBIC = 0.044715
MESH = pl.DeviceIdType.MESH
BF = jnp.bfloat16
F32 = jnp.float32
VMEM_LIMIT = 48 << 20


def coords():
    row, col = lax.axis_index("row"), lax.axis_index("col")
    return row % 4, col // 4, row // 4, (col // 2) % 2, col % 2


def dev(x, y, zl, zh, c):
    return (zl * 4 + x, y * 4 + zh * 2 + c)


def unit(y, zh, c):
    return y * 4 + zh * 2 + c


def remote(src, dst, ss, rs, to):
    return pltpu.make_async_remote_copy(
        src_ref=src, dst_ref=dst, send_sem=ss, recv_sem=rs, device_id=to, device_id_type=MESH
    )


def greet(x, y, zl, zh, c):
    barrier = pltpu.get_barrier_semaphore()

    def hello(to):
        pl.semaphore_signal(barrier, inc=1, device_id=to, device_id_type=MESH)

    for i in range(1, 4):
        hello(dev((x + i) % 4, y, zl, zh, c))
        hello(dev(x, (y + i) % 4, zl, zh, c))
    hello(dev(x, y, zl, 1 - zh, c))
    hello(dev(x, y, zl, zh, 1 - c))

    hello(dev(x, y, (zl + 1) % 8, jnp.where(zl == NZ - 1, 1 - zh, zh), c))
    hello(dev(x, y, (zl + 7) % 8, jnp.where(zl == 0, 1 - zh, zh), c))
    pl.semaphore_wait(barrier, 10)


def gather_kernel(
    tok, grad, wup, wdn, uf, uh, uc, df, dh, dc,
    T, W, C,
    t_send, t_recv, wz_send, wz_recv, wx_send, wx_recv, cz_send, cz_recv, cx_send, cx_recv,
):
    x, y, zl, zh, c = coords()
    me = unit(y, zh, c)
    lane = lax.broadcasted_iota(jnp.int32, (1, 128), 1)
    code = jnp.zeros((1, 128), jnp.int32)
    for base, ref in ((0, uf), (4, uh), (8, df), (12, dh)):
        for s in range(CAP):
            code = jnp.where(lane == base + s, ref[0, s], code)
    C[x, zl] = code
    slot = lax.broadcasted_iota(jnp.int32, (BLK, CAP * BLK), 1) // BLK
    zero = jnp.zeros((BLK, CAP * BLK), F32)
    W[x, zl, 0:BLK] = jnp.where(slot < uc[0, 0], wup[...].astype(F32), zero).astype(BF)
    W[x, zl, BLK : 2 * BLK] = jnp.where(slot < dc[0, 0], wdn[...].astype(F32), zero).astype(BF)
    T[0, me] = tok[...].astype(F32).T.astype(BF)
    T[1, me] = grad[...].astype(F32).T.astype(BF)
    greet(x, y, zl, zh, c)

    def chain(way, j):
        to = dev(x, y, zl + (1 if way == 0 else -1), zh, c)
        return (
            remote(C.at[x, j], C.at[x, j], cz_send.at[way, j], cz_recv.at[j], to),
            remote(W.at[x, j], W.at[x, j], wz_send.at[way, j], wz_recv.at[j], to),
        )

    def chain_start(way, j):
        @pl.when((zl < NZ - 1) if way == 0 else (zl > 0))
        def _():
            for cp in chain(way, j):
                cp.start()

    def spread(j, i):
        to = dev((x + i) % 4, y, zl, zh, c)
        return remote(W.at[x, j], W.at[x, j], wx_send.at[j, i], wx_recv.at[x, j], to)

    def spread_start(j):
        for i in (1, 3, 2):
            spread(j, i).start()

    def sends(a, u):
        first = unit(y, zh, c)
        base = jnp.where(u == first, 0, 4)
        out = []
        for n, i in enumerate((1, 3, 2)):
            to = dev(x, (y + i) % 4, zl, zh, c)
            out.append(remote(T.at[a, u], T.at[a, u], t_send.at[a, base + n], t_recv.at[a, u], to))
        return out

    def core_send(a, u, n):
        return remote(
            T.at[a, u], T.at[a, u], t_send.at[a, 8 + n], t_recv.at[a, u], dev(x, y, zl, zh, 1 - c)
        )

    def z_send(a):
        return remote(
            T.at[a, me], T.at[a, me], t_send.at[a, 3], t_recv.at[a, me], dev(x, y, zl, 1 - zh, c)
        )

    def t_wait(a, u):
        remote(T.at[a, u], T.at[a, u], t_send.at[a, 7], t_recv.at[a, u], dev(x, y, zl, zh, 1 - c)).wait_recv()

    chain_start(0, zl)
    chain_start(1, zl)
    z_send(0).start()
    spread_start(zl)
    for cp in sends(0, me):
        cp.start()
    core_send(0, me, 0).start()
    z_send(1).start()
    for cp in sends(1, me):
        cp.start()
    core_send(1, me, 0).start()
    other = unit(y, 1 - zh, c)

    def near(a):
        for n, i in enumerate((1, 3, 2)):
            u = unit((y + i) % 4, zh, c)
            t_wait(a, u)
            core_send(a, u, 2 + n).start()

    def partner(a):
        t_wait(a, other)
        for cp in sends(a, other):
            cp.start()
        core_send(a, other, 1).start()

    def far(a):
        for n, i in enumerate((1, 3, 2)):
            u = unit((y + i) % 4, 1 - zh, c)
            t_wait(a, u)
            core_send(a, u, 5 + n).start()

    def step(t):
        @pl.when(zl - t >= 0)
        def _():
            j = zl - t
            for cp in chain(0, j):
                cp.wait_recv()
            chain_start(0, j)
            spread_start(j)

        @pl.when(zl + t <= NZ - 1)
        def _():
            j = zl + t
            for cp in chain(1, j):
                cp.wait_recv()
            chain_start(1, j)
            spread_start(j)

    step(1)
    step(2)
    near(0)
    step(3)
    step(4)
    partner(0)
    near(1)
    step(5)
    step(6)
    far(0)
    step(7)

    def code_send(i):
        to = dev((x + i) % 4, y, zl, zh, c)
        return remote(C.at[x], C.at[x], cx_send.at[i], cx_recv.at[x], to)

    for i in range(1, 4):
        code_send(i).start()
    partner(1)
    far(1)
    for i in range(1, 4):
        xs = (x + i) % 4
        to = dev(xs, y, zl, zh, c)
        remote(C.at[xs], C.at[xs], cx_send.at[i], cx_recv.at[xs], to).wait_recv()

        @pl.loop(0, NZ)
        def _(j):
            remote(W.at[xs, j], W.at[xs, j], wx_send.at[j, i], wx_recv.at[xs, j], to).wait_recv()

    for a in range(2):
        for u in range(8):
            t_wait(a, 2 * u + 1 - c)
    for i in range(1, 4):
        code_send(i).wait_send()

        @pl.loop(0, NZ)
        def _(j):
            spread(j, i).wait_send()

    @pl.loop(0, NZ)
    def _(j):
        @pl.when((j <= zl) & (zl < NZ - 1))
        def _():
            for cp in chain(0, j):
                cp.wait_send()

        @pl.when((j >= zl) & (zl > 0))
        def _():
            for cp in chain(1, j):
                cp.wait_send()

    for a in range(2):
        z_send(a).wait_send()
        for u in (me, other):
            for cp in sends(a, u):
                cp.wait_send()
        for n in range(8):
            core_send(a, me, n).wait_send()


def gelu_parts(v):
    t = jnp.tanh(GELU_SCALE * (v + GELU_CUBIC * v * v * v))
    values = 0.5 * v * (1.0 + t)
    slope = 0.5 * (1.0 + t) + 0.5 * v * (1.0 - t * t) * GELU_SCALE * (1.0 + 3.0 * GELU_CUBIC * v * v)
    return values, slope


def dot(a, b):
    return jnp.dot(a, b, preferred_element_type=F32)


def dot_nt(a, b):
    return lax.dot_general(a, b, (((1,), (1,)), ((), ())), preferred_element_type=F32)


def compute_kernel(T, W, C, M, G, hid, back, act, slope, gp, acc):
    hid[...] = jnp.zeros_like(hid)
    back[...] = jnp.zeros_like(back)

    def code(r, base, s):
        return C[r % 4, r // 4, 0, base + s]

    @pl.loop(0, ROWS, unroll=2)
    def _(r):
        wt = W[r % 4, r // 4, 0:BLK].astype(F32).T.astype(BF)
        for s in range(CAP):
            o = dot(wt[s * BLK : (s + 1) * BLK], T[0, r * 3 + code(r, 0, s)])
            h = code(r, 4, s)
            hid[h] = hid[h] + o

    @pl.loop(0, HB)
    def _(k):
        v, d = gelu_parts(hid[k])
        act[k] = v.astype(BF)
        slope[k] = d

    @pl.loop(0, ROWS, unroll=2)
    def _(r):
        w = W[r % 4, r // 4, BLK : 2 * BLK]
        wt = w.astype(F32).T.astype(BF)
        acc[...] = jnp.zeros_like(acc)
        grads = []
        for s in range(CAP):
            f, h = code(r, 8, s), code(r, 12, s)
            active, out = act[h], T[1, r * 3 + f]
            acc[f] = acc[f] + dot(wt[s * BLK : (s + 1) * BLK], active)
            back[h] = back[h] + dot(w[:, s * BLK : (s + 1) * BLK], out)
            grads.append(dot_nt(active, out))
        G[r % 4, r // 4, BLK : 2 * BLK] = jnp.concatenate(grads, axis=1).astype(BF)
        for f in range(3):
            M[0, r * 3 + f] = acc[f].astype(BF)

    @pl.loop(0, HB)
    def _(k):
        gp[k] = (back[k] * slope[k]).astype(BF)

    @pl.loop(0, ROWS, unroll=2)
    def _(r):
        w = W[r % 4, r // 4, 0:BLK]
        acc[...] = jnp.zeros_like(acc)
        grads = []
        for s in range(CAP):
            f, h = code(r, 0, s), code(r, 4, s)
            g = gp[h]
            acc[f] = acc[f] + dot(w[:, s * BLK : (s + 1) * BLK], g)
            grads.append(dot_nt(T[0, r * 3 + f], g))
        G[r % 4, r // 4, 0:BLK] = jnp.concatenate(grads, axis=1).astype(BF)
        for f in range(3):
            M[1, r * 3 + f] = acc[f].astype(BF)


def scatter_kernel(
    M, G, uc, dc,
    mixed, gin, gup, gdn,
    rc, s1, ry, s2, rz, rx, sz, rl, rr,
    c_send, c_recv, y_send, y_recv, z_send, z_recv, x_send, x_recv, l_send, l_recv, r_send, r_recv,
):
    x, y, zl, zh, c = coords()
    greet(x, y, zl, zh, c)

    def xs(j, i):
        xt = (x + i) % 4
        return remote(G.at[xt, j], rx.at[i - 1, j], x_send.at[j, i], x_recv.at[j, i], dev(xt, y, zl, zh, c))

    def cs(a, u):
        return remote(
            M.at[a, 2 * u + 1 - c], rc.at[a, u], c_send.at[a, u], c_recv.at[a, u], dev(x, y, zl, zh, 1 - c)
        )

    def ys(a, i, h):
        yt = (y + i) % 4
        return remote(
            s1.at[a, yt * 2 + h], ry.at[a, i - 1, h], y_send.at[a, i - 1, h], y_recv.at[a, i - 1, h],
            dev(x, yt, zl, zh, c),
        )

    def zs(a):
        return remote(s2.at[a], rz.at[a], z_send.at[a], z_recv.at[a], dev(x, y, zl, 1 - zh, c))

    for j in (0, 7):
        for i in (1, 3, 2):
            xs(j, i).start()
    for a in range(2):
        for u in range(8):
            cs(a, u).start()
    for j in (1, 6, 2, 5, 3, 4):
        for i in (1, 3, 2):
            xs(j, i).start()

    def add_core(a, u):
        cs(a, u).wait_recv()
        s1[a, u] = (M[a, 2 * u + c].astype(F32) + rc[a, u].astype(F32)).astype(BF)

    def core_stage(a):
        for h in (0, 1):
            hh = jnp.where(h == 0, 1 - zh, zh)
            for i in (1, 3, 2):
                add_core(a, ((y + i) % 4) * 2 + hh)
                ys(a, i, hh).start()
        for h in range(2):
            add_core(a, y * 2 + h)

    def y_sum(a, h):
        for i in range(1, 4):
            ys(a, i, h).wait_recv()
        total = s1[a, y * 2 + h].astype(F32)
        for i in range(3):
            total = total + ry[a, i, h].astype(F32)
        return total

    def y_stage(a):
        s2[a] = y_sum(a, 1 - zh).astype(BF)
        zs(a).start()

    def z_stage(a, out):
        own = y_sum(a, zh)
        zs(a).wait_recv()
        out[...] = (own + rz[a].astype(F32)).T.astype(BF)

    def x_sum(j):
        for i in range(1, 4):
            xs(j, i).wait_recv()
        total = G[x, j].astype(F32)
        for i in range(3):
            total = total + rx[i, j].astype(F32)
        return total

    def left(j):
        return remote(sz.at[j], rl.at[j], l_send.at[j], l_recv.at[j], dev(x, y, zl - 1, zh, c))

    def right(j):
        return remote(sz.at[j], rr.at[j], r_send.at[j], r_recv.at[j], dev(x, y, zl + 1, zh, c))

    def step(t):
        @pl.when(t < zl)
        def _():
            total = x_sum(t)

            @pl.when(zl < NZ - 1)
            def _():
                left(t).wait_recv()
                sz[t] = (total + rl[t].astype(F32)).astype(BF)

            @pl.when(zl == NZ - 1)
            def _():
                sz[t] = total.astype(BF)

            left(t).start()

        j = NZ - 1 - t

        @pl.when(j > zl)
        def _():
            total = x_sum(j)

            @pl.when(zl > 0)
            def _():
                right(j).wait_recv()
                sz[j] = (total + rr[j].astype(F32)).astype(BF)

            @pl.when(zl == 0)
            def _():
                sz[j] = total.astype(BF)

            right(j).start()

    core_stage(0)
    core_stage(1)
    step(0)
    y_stage(0)
    step(1)
    step(2)
    y_stage(1)
    for t in range(3, 7):
        step(t)
    own = x_sum(zl)

    @pl.when(zl < NZ - 1)
    def _():
        left(zl).wait_recv()

    @pl.when(zl > 0)
    def _():
        right(zl).wait_recv()

    from_left = jnp.where(zl > 0, rr[zl].astype(F32), 0.0)
    from_right = jnp.where(zl < NZ - 1, rl[zl].astype(F32), 0.0)
    own = own + from_left + from_right
    slot = lax.broadcasted_iota(jnp.int32, (BLK, CAP * BLK), 1) // BLK
    gup[...] = jnp.where(slot < uc[0, 0], own[0:BLK], 0.0).astype(BF)
    gdn[...] = jnp.where(slot < dc[0, 0], own[BLK : 2 * BLK], 0.0).astype(BF)
    z_stage(0, mixed)
    z_stage(1, gin)

    for a in range(2):
        zs(a).wait_send()
        for u in range(8):
            cs(a, u).wait_send()
        for i in range(1, 4):
            for h in range(2):
                ys(a, i, h).wait_send()

    @pl.loop(0, NZ)
    def _(j):
        for i in range(1, 4):
            xs(j, i).wait_send()

        @pl.when(j < zl)
        def _():
            left(j).wait_send()

        @pl.when(j > zl)
        def _():
            right(j).wait_send()


def vmem():
    return pl.BlockSpec(memory_space=pltpu.VMEM)


def smem():
    return pl.BlockSpec(memory_space=pltpu.SMEM)


def shards(tokens, w_up, up_feat, up_hid, up_count, w_down, down_feat, down_hid, down_count, grad_out):
    dma = pltpu.SemaphoreType.DMA
    T, W, C = pl.pallas_call(
        gather_kernel,
        name="gather",
        out_shape=(
            jax.ShapeDtypeStruct((2, UNITS, FEAT, TOK), BF),
            jax.ShapeDtypeStruct((NX, NZ, 2 * BLK, CAP * BLK), BF),
            jax.ShapeDtypeStruct((NX, NZ, 1, 128), jnp.int32),
        ),
        in_specs=[vmem()] * 4 + [smem()] * 6,
        out_specs=(vmem(),) * 3,
        scratch_shapes=[
            dma((2, 16)), dma((2, 16)), dma((2, 8)), dma((8,)), dma((8, 4)), dma((4, 8)),
            dma((2, 8)), dma((8,)), dma((4,)), dma((4,)),
        ],
        compiler_params=pltpu.CompilerParams(
            collective_id=0, has_side_effects=True, vmem_limit_bytes=VMEM_LIMIT
        ),
    )(tokens, grad_out, w_up, w_down, up_feat, up_hid, up_count, down_feat, down_hid, down_count)
    M, G = pl.pallas_call(
        compute_kernel,
        name="compute",
        out_shape=(
            jax.ShapeDtypeStruct((2, UNITS * FEAT // BLK, BLK, TOK), BF),
            jax.ShapeDtypeStruct((NX, NZ, 2 * BLK, CAP * BLK), BF),
        ),
        in_specs=[vmem(), vmem(), smem()],
        out_specs=(vmem(), vmem()),
        scratch_shapes=[
            pltpu.VMEM((HB, BLK, TOK), F32),
            pltpu.VMEM((HB, BLK, TOK), F32),
            pltpu.VMEM((HB, BLK, TOK), BF),
            pltpu.VMEM((HB, BLK, TOK), F32),
            pltpu.VMEM((HB, BLK, TOK), BF),
            pltpu.VMEM((3, BLK, TOK), F32),
        ],
        compiler_params=pltpu.CompilerParams(vmem_limit_bytes=VMEM_LIMIT),
    )(T.reshape(2, UNITS * FEAT // BLK, BLK, TOK), W, C)
    tile = (2 * BLK, CAP * BLK)
    return pl.pallas_call(
        scatter_kernel,
        name="scatter",
        out_shape=(
            jax.ShapeDtypeStruct((TOK, FEAT), BF),
            jax.ShapeDtypeStruct((TOK, FEAT), BF),
            jax.ShapeDtypeStruct((BLK, CAP * BLK), BF),
            jax.ShapeDtypeStruct((BLK, CAP * BLK), BF),
        ),
        in_specs=[vmem(), vmem(), smem(), smem()],
        out_specs=(vmem(),) * 4,
        scratch_shapes=[
            pltpu.VMEM((2, 8, FEAT, TOK), BF),
            pltpu.VMEM((2, 8, FEAT, TOK), BF),
            pltpu.VMEM((2, 3, 2, FEAT, TOK), BF),
            pltpu.VMEM((2, FEAT, TOK), BF),
            pltpu.VMEM((2, FEAT, TOK), BF),
            pltpu.VMEM((3, NZ) + tile, BF),
            pltpu.VMEM((NZ,) + tile, BF),
            pltpu.VMEM((NZ,) + tile, BF),
            pltpu.VMEM((NZ,) + tile, BF),
            dma((2, 8)), dma((2, 8)), dma((2, 3, 2)), dma((2, 3, 2)), dma((2,)), dma((2,)),
            dma((8, 4)), dma((8, 4)), dma((8,)), dma((8,)), dma((8,)), dma((8,)),
        ],
        compiler_params=pltpu.CompilerParams(
            collective_id=1, has_side_effects=True, vmem_limit_bytes=VMEM_LIMIT
        ),
    )(M.reshape(2, UNITS, FEAT, TOK), G, up_count, down_count)


def solution(mesh):
    return jax.shard_map(
        shards,
        mesh=mesh,
        in_specs=(P("row", "col"),) * 10,
        out_specs=(P("row", "col"),) * 4,
        check_vma=False,
    )
```

```python
import jax
import jax.numpy as jnp
from jax import lax
from jax.experimental import pallas as pl
from jax.experimental.pallas import tpu as pltpu
from jax.sharding import PartitionSpec as P

BLK = 64
CAP = 4
TOK = 128
FEAT = 384
HB = 24
NX, NY, NZ = 4, 4, 8
UNITS = 16
ROWS = 32
GELU_SCALE = 0.7978845608028654
GELU_CUBIC = 0.044715
MESH = pl.DeviceIdType.MESH
BF = jnp.bfloat16
F32 = jnp.float32
VMEM_LIMIT = 48 << 20


def coords():
    row, col = lax.axis_index("row"), lax.axis_index("col")
    return row % 4, col // 4, row // 4, (col // 2) % 2, col % 2


def dev(x, y, zl, zh, c):
    return (zl * 4 + x, y * 4 + zh * 2 + c)


def unit(y, zh, c):
    return y * 4 + zh * 2 + c


def remote(src, dst, ss, rs, to):
    return pltpu.make_async_remote_copy(
        src_ref=src, dst_ref=dst, send_sem=ss, recv_sem=rs, device_id=to, device_id_type=MESH
    )


def greet(x, y, zl, zh, c):
    barrier = pltpu.get_barrier_semaphore()

    def hello(to):
        pl.semaphore_signal(barrier, inc=1, device_id=to, device_id_type=MESH)

    for i in range(1, 4):
        hello(dev((x + i) % 4, y, zl, zh, c))
        hello(dev(x, (y + i) % 4, zl, zh, c))
    hello(dev(x, y, zl, 1 - zh, c))
    hello(dev(x, y, zl, zh, 1 - c))

    hello(dev(x, y, (zl + 1) % 8, jnp.where(zl == NZ - 1, 1 - zh, zh), c))
    hello(dev(x, y, (zl + 7) % 8, jnp.where(zl == 0, 1 - zh, zh), c))
    pl.semaphore_wait(barrier, 10)


def gather_kernel(
    tok, grad, wup, wdn, uf, uh, uc, df, dh, dc,
    T, W, C,
    t_send, t_recv, wz_send, wz_recv, wx_send, wx_recv, cz_send, cz_recv, cx_send, cx_recv,
):
    x, y, zl, zh, c = coords()
    me = unit(y, zh, c)
    lane = lax.broadcasted_iota(jnp.int32, (1, 128), 1)
    code = jnp.zeros((1, 128), jnp.int32)
    for base, ref in ((0, uf), (4, uh), (8, df), (12, dh)):
        for s in range(CAP):
            code = jnp.where(lane == base + s, ref[0, s], code)
    C[x, zl] = code
    slot = lax.broadcasted_iota(jnp.int32, (BLK, CAP * BLK), 1) // BLK
    zero = jnp.zeros((BLK, CAP * BLK), F32)
    W[x, zl, 0:BLK] = jnp.where(slot < uc[0, 0], wup[...].astype(F32), zero).astype(BF)
    W[x, zl, BLK : 2 * BLK] = jnp.where(slot < dc[0, 0], wdn[...].astype(F32), zero).astype(BF)
    T[0, me] = tok[...].astype(F32).T.astype(BF)
    T[1, me] = grad[...].astype(F32).T.astype(BF)
    greet(x, y, zl, zh, c)

    def chain(way, j):
        to = dev(x, y, zl + (1 if way == 0 else -1), zh, c)
        return (
            remote(C.at[x, j], C.at[x, j], cz_send.at[way, j], cz_recv.at[j], to),
            remote(W.at[x, j], W.at[x, j], wz_send.at[way, j], wz_recv.at[j], to),
        )

    def chain_start(way, j):
        @pl.when((zl < NZ - 1) if way == 0 else (zl > 0))
        def _():
            for cp in chain(way, j):
                cp.start()

    def spread(j, i):
        to = dev((x + i) % 4, y, zl, zh, c)
        return remote(W.at[x, j], W.at[x, j], wx_send.at[j, i], wx_recv.at[x, j], to)

    def spread_start(j):
        for i in (1, 3, 2):
            spread(j, i).start()

    def sends(a, u):
        first = unit(y, zh, c)
        base = jnp.where(u == first, 0, 4)
        out = []
        for n, i in enumerate((1, 3, 2)):
            to = dev(x, (y + i) % 4, zl, zh, c)
            out.append(remote(T.at[a, u], T.at[a, u], t_send.at[a, base + n], t_recv.at[a, u], to))
        return out

    def core_send(a, u, n):
        return remote(
            T.at[a, u], T.at[a, u], t_send.at[a, 8 + n], t_recv.at[a, u], dev(x, y, zl, zh, 1 - c)
        )

    def z_send(a):
        return remote(
            T.at[a, me], T.at[a, me], t_send.at[a, 3], t_recv.at[a, me], dev(x, y, zl, 1 - zh, c)
        )

    def t_wait(a, u):
        remote(T.at[a, u], T.at[a, u], t_send.at[a, 7], t_recv.at[a, u], dev(x, y, zl, zh, 1 - c)).wait_recv()

    chain_start(0, zl)
    chain_start(1, zl)
    z_send(0).start()
    spread_start(zl)
    for cp in sends(0, me):
        cp.start()
    core_send(0, me, 0).start()
    z_send(1).start()
    for cp in sends(1, me):
        cp.start()
    core_send(1, me, 0).start()
    other = unit(y, 1 - zh, c)

    def near(a):
        for n, i in enumerate((1, 3, 2)):
            u = unit((y + i) % 4, zh, c)
            t_wait(a, u)
            core_send(a, u, 2 + n).start()

    def partner(a):
        t_wait(a, other)
        for cp in sends(a, other):
            cp.start()
        core_send(a, other, 1).start()

    def far(a):
        for n, i in enumerate((1, 3, 2)):
            u = unit((y + i) % 4, 1 - zh, c)
            t_wait(a, u)
            core_send(a, u, 5 + n).start()

    def step(t):
        @pl.when(zl - t >= 0)
        def _():
            j = zl - t
            for cp in chain(0, j):
                cp.wait_recv()
            chain_start(0, j)
            spread_start(j)

        @pl.when(zl + t <= NZ - 1)
        def _():
            j = zl + t
            for cp in chain(1, j):
                cp.wait_recv()
            chain_start(1, j)
            spread_start(j)

    step(1)
    step(2)
    near(0)
    step(3)
    step(4)
    partner(0)
    near(1)
    step(5)
    step(6)
    far(0)
    step(7)

    def code_send(i):
        to = dev((x + i) % 4, y, zl, zh, c)
        return remote(C.at[x], C.at[x], cx_send.at[i], cx_recv.at[x], to)

    for i in range(1, 4):
        code_send(i).start()
    partner(1)
    far(1)
    for i in range(1, 4):
        xs = (x + i) % 4
        to = dev(xs, y, zl, zh, c)
        remote(C.at[xs], C.at[xs], cx_send.at[i], cx_recv.at[xs], to).wait_recv()

        @pl.loop(0, NZ)
        def _(j):
            remote(W.at[xs, j], W.at[xs, j], wx_send.at[j, i], wx_recv.at[xs, j], to).wait_recv()

    for a in range(2):
        for u in range(8):
            t_wait(a, 2 * u + 1 - c)
    for i in range(1, 4):
        code_send(i).wait_send()

        @pl.loop(0, NZ)
        def _(j):
            spread(j, i).wait_send()

    @pl.loop(0, NZ)
    def _(j):
        @pl.when((j <= zl) & (zl < NZ - 1))
        def _():
            for cp in chain(0, j):
                cp.wait_send()

        @pl.when((j >= zl) & (zl > 0))
        def _():
            for cp in chain(1, j):
                cp.wait_send()

    for a in range(2):
        z_send(a).wait_send()
        for u in (me, other):
            for cp in sends(a, u):
                cp.wait_send()
        for n in range(8):
            core_send(a, me, n).wait_send()


def gelu_parts(v):
    t = jnp.tanh(GELU_SCALE * (v + GELU_CUBIC * v * v * v))
    values = 0.5 * v * (1.0 + t)
    slope = 0.5 * (1.0 + t) + 0.5 * v * (1.0 - t * t) * GELU_SCALE * (1.0 + 3.0 * GELU_CUBIC * v * v)
    return values, slope


def dot(a, b):
    return jnp.dot(a, b, preferred_element_type=F32)


def dot_nt(a, b):
    return lax.dot_general(a, b, (((1,), (1,)), ((), ())), preferred_element_type=F32)


def compute_kernel(T, W, C, M, G, hid, back, act, slope, gp, acc):
    hid[...] = jnp.zeros_like(hid)
    back[...] = jnp.zeros_like(back)

    def code(r, base, s):
        return C[r % 4, r // 4, 0, base + s]

    @pl.loop(0, ROWS, unroll=2)
    def _(r):
        wt = W[r % 4, r // 4, 0:BLK].astype(F32).T.astype(BF)
        for s in range(CAP):
            o = dot(wt[s * BLK : (s + 1) * BLK], T[0, r * 3 + code(r, 0, s)])
            h = code(r, 4, s)
            hid[h] = hid[h] + o

    @pl.loop(0, HB)
    def _(k):
        v, d = gelu_parts(hid[k])
        act[k] = v.astype(BF)
        slope[k] = d

    @pl.loop(0, ROWS, unroll=2)
    def _(r):
        w = W[r % 4, r // 4, BLK : 2 * BLK]
        wt = w.astype(F32).T.astype(BF)
        acc[...] = jnp.zeros_like(acc)
        grads = []
        for s in range(CAP):
            f, h = code(r, 8, s), code(r, 12, s)
            active, out = act[h], T[1, r * 3 + f]
            acc[f] = acc[f] + dot(wt[s * BLK : (s + 1) * BLK], active)
            back[h] = back[h] + dot(w[:, s * BLK : (s + 1) * BLK], out)
            grads.append(dot_nt(active, out))
        G[r % 4, r // 4, BLK : 2 * BLK] = jnp.concatenate(grads, axis=1).astype(BF)
        for f in range(3):
            M[0, r * 3 + f] = acc[f].astype(BF)

    @pl.loop(0, HB)
    def _(k):
        gp[k] = (back[k] * slope[k]).astype(BF)

    @pl.loop(0, ROWS, unroll=2)
    def _(r):
        w = W[r % 4, r // 4, 0:BLK]
        acc[...] = jnp.zeros_like(acc)
        grads = []
        for s in range(CAP):
            f, h = code(r, 0, s), code(r, 4, s)
            g = gp[h]
            acc[f] = acc[f] + dot(w[:, s * BLK : (s + 1) * BLK], g)
            grads.append(dot_nt(T[0, r * 3 + f], g))
        G[r % 4, r // 4, 0:BLK] = jnp.concatenate(grads, axis=1).astype(BF)
        for f in range(3):
            M[1, r * 3 + f] = acc[f].astype(BF)


def scatter_kernel(
    M, G, uc, dc,
    mixed, gin, gup, gdn,
    rc, s1, ry, s2, rz, rx, sz, rl, rr,
    c_send, c_recv, y_send, y_recv, z_send, z_recv, x_send, x_recv, l_send, l_recv, r_send, r_recv,
):
    x, y, zl, zh, c = coords()
    greet(x, y, zl, zh, c)

    def xs(j, i):
        xt = (x + i) % 4
        return remote(G.at[xt, j], rx.at[i - 1, j], x_send.at[j, i], x_recv.at[j, i], dev(xt, y, zl, zh, c))

    def cs(a, u):
        return remote(
            M.at[a, 2 * u + 1 - c], rc.at[a, u], c_send.at[a, u], c_recv.at[a, u], dev(x, y, zl, zh, 1 - c)
        )

    def ys(a, i, h):
        yt = (y + i) % 4
        return remote(
            s1.at[a, yt * 2 + h], ry.at[a, i - 1, h], y_send.at[a, i - 1, h], y_recv.at[a, i - 1, h],
            dev(x, yt, zl, zh, c),
        )

    def zs(a):
        return remote(s2.at[a], rz.at[a], z_send.at[a], z_recv.at[a], dev(x, y, zl, 1 - zh, c))

    def x_start(t):
        @pl.when(t >= NZ - 1 - zl)
        def _():
            for i in (1, 3, 2):
                xs(t - NZ + 1 + zl, i).start()

        @pl.when(t >= zl)
        def _():
            for i in (1, 3, 2):
                xs(NZ - 1 - t + zl, i).start()

    x_start(0)
    x_start(1)
    for u in range(8):
        cs(0, u).start()
    x_start(2)
    x_start(3)
    for u in range(8):
        cs(1, u).start()
    for t in range(4, 7):
        x_start(t)
    for i in (1, 3, 2):
        xs(zl, i).start()

    def add_core(a, u):
        cs(a, u).wait_recv()
        s1[a, u] = (M[a, 2 * u + c].astype(F32) + rc[a, u].astype(F32)).astype(BF)

    def core_stage(a):
        for h in (0, 1):
            hh = jnp.where(h == 0, 1 - zh, zh)
            for i in (1, 3, 2):
                add_core(a, ((y + i) % 4) * 2 + hh)
                ys(a, i, hh).start()
        for h in range(2):
            add_core(a, y * 2 + h)

    def y_sum(a, h):
        for i in range(1, 4):
            ys(a, i, h).wait_recv()
        total = s1[a, y * 2 + h].astype(F32)
        for i in range(3):
            total = total + ry[a, i, h].astype(F32)
        return total

    def y_stage(a):
        s2[a] = y_sum(a, 1 - zh).astype(BF)
        zs(a).start()

    def z_stage(a, out):
        own = y_sum(a, zh)
        zs(a).wait_recv()
        out[...] = (own + rz[a].astype(F32)).T.astype(BF)

    def x_sum(j):
        for i in range(1, 4):
            xs(j, i).wait_recv()
        total = G[x, j].astype(F32)
        for i in range(3):
            total = total + rx[i, j].astype(F32)
        return total

    def left(j):
        return remote(sz.at[j], rl.at[j], l_send.at[j], l_recv.at[j], dev(x, y, zl - 1, zh, c))

    def right(j):
        return remote(sz.at[j], rr.at[j], r_send.at[j], r_recv.at[j], dev(x, y, zl + 1, zh, c))

    def step(t):
        @pl.when(t >= NZ - 1 - zl)
        def _():
            j = t - NZ + 1 + zl
            total = x_sum(j)

            @pl.when(zl < NZ - 1)
            def _():
                left(j).wait_recv()
                sz[j] = (total + rl[j].astype(F32)).astype(BF)

            @pl.when(zl == NZ - 1)
            def _():
                sz[j] = total.astype(BF)

            left(j).start()

        @pl.when(t >= zl)
        def _():
            j = NZ - 1 - t + zl
            total = x_sum(j)

            @pl.when(zl > 0)
            def _():
                right(j).wait_recv()
                sz[j] = (total + rr[j].astype(F32)).astype(BF)

            @pl.when(zl == 0)
            def _():
                sz[j] = total.astype(BF)

            right(j).start()

    core_stage(0)
    core_stage(1)
    step(0)
    y_stage(0)
    step(1)
    step(2)
    y_stage(1)
    for t in range(3, 7):
        step(t)
    own = x_sum(zl)

    @pl.when(zl < NZ - 1)
    def _():
        left(zl).wait_recv()

    @pl.when(zl > 0)
    def _():
        right(zl).wait_recv()

    from_left = jnp.where(zl > 0, rr[zl].astype(F32), 0.0)
    from_right = jnp.where(zl < NZ - 1, rl[zl].astype(F32), 0.0)
    own = own + from_left + from_right
    slot = lax.broadcasted_iota(jnp.int32, (BLK, CAP * BLK), 1) // BLK
    gup[...] = jnp.where(slot < uc[0, 0], own[0:BLK], 0.0).astype(BF)
    gdn[...] = jnp.where(slot < dc[0, 0], own[BLK : 2 * BLK], 0.0).astype(BF)
    z_stage(0, mixed)
    z_stage(1, gin)

    for a in range(2):
        zs(a).wait_send()
        for u in range(8):
            cs(a, u).wait_send()
        for i in range(1, 4):
            for h in range(2):
                ys(a, i, h).wait_send()

    @pl.loop(0, NZ)
    def _(j):
        for i in range(1, 4):
            xs(j, i).wait_send()

        @pl.when(j < zl)
        def _():
            left(j).wait_send()

        @pl.when(j > zl)
        def _():
            right(j).wait_send()


def vmem():
    return pl.BlockSpec(memory_space=pltpu.VMEM)


def smem():
    return pl.BlockSpec(memory_space=pltpu.SMEM)


def shards(tokens, w_up, up_feat, up_hid, up_count, w_down, down_feat, down_hid, down_count, grad_out):
    dma = pltpu.SemaphoreType.DMA
    T, W, C = pl.pallas_call(
        gather_kernel,
        name="gather",
        out_shape=(
            jax.ShapeDtypeStruct((2, UNITS, FEAT, TOK), BF),
            jax.ShapeDtypeStruct((NX, NZ, 2 * BLK, CAP * BLK), BF),
            jax.ShapeDtypeStruct((NX, NZ, 1, 128), jnp.int32),
        ),
        in_specs=[vmem()] * 4 + [smem()] * 6,
        out_specs=(vmem(),) * 3,
        scratch_shapes=[
            dma((2, 16)), dma((2, 16)), dma((2, 8)), dma((8,)), dma((8, 4)), dma((4, 8)),
            dma((2, 8)), dma((8,)), dma((4,)), dma((4,)),
        ],
        compiler_params=pltpu.CompilerParams(
            collective_id=0, has_side_effects=True, vmem_limit_bytes=VMEM_LIMIT
        ),
    )(tokens, grad_out, w_up, w_down, up_feat, up_hid, up_count, down_feat, down_hid, down_count)
    M, G = pl.pallas_call(
        compute_kernel,
        name="compute",
        out_shape=(
            jax.ShapeDtypeStruct((2, UNITS * FEAT // BLK, BLK, TOK), BF),
            jax.ShapeDtypeStruct((NX, NZ, 2 * BLK, CAP * BLK), BF),
        ),
        in_specs=[vmem(), vmem(), smem()],
        out_specs=(vmem(), vmem()),
        scratch_shapes=[
            pltpu.VMEM((HB, BLK, TOK), F32),
            pltpu.VMEM((HB, BLK, TOK), F32),
            pltpu.VMEM((HB, BLK, TOK), BF),
            pltpu.VMEM((HB, BLK, TOK), F32),
            pltpu.VMEM((HB, BLK, TOK), BF),
            pltpu.VMEM((3, BLK, TOK), F32),
        ],
        compiler_params=pltpu.CompilerParams(vmem_limit_bytes=VMEM_LIMIT),
    )(T.reshape(2, UNITS * FEAT // BLK, BLK, TOK), W, C)
    tile = (2 * BLK, CAP * BLK)
    return pl.pallas_call(
        scatter_kernel,
        name="scatter",
        out_shape=(
            jax.ShapeDtypeStruct((TOK, FEAT), BF),
            jax.ShapeDtypeStruct((TOK, FEAT), BF),
            jax.ShapeDtypeStruct((BLK, CAP * BLK), BF),
            jax.ShapeDtypeStruct((BLK, CAP * BLK), BF),
        ),
        in_specs=[vmem(), vmem(), smem(), smem()],
        out_specs=(vmem(),) * 4,
        scratch_shapes=[
            pltpu.VMEM((2, 8, FEAT, TOK), BF),
            pltpu.VMEM((2, 8, FEAT, TOK), BF),
            pltpu.VMEM((2, 3, 2, FEAT, TOK), BF),
            pltpu.VMEM((2, FEAT, TOK), BF),
            pltpu.VMEM((2, FEAT, TOK), BF),
            pltpu.VMEM((3, NZ) + tile, BF),
            pltpu.VMEM((NZ,) + tile, BF),
            pltpu.VMEM((NZ,) + tile, BF),
            pltpu.VMEM((NZ,) + tile, BF),
            dma((2, 8)), dma((2, 8)), dma((2, 3, 2)), dma((2, 3, 2)), dma((2,)), dma((2,)),
            dma((8, 4)), dma((8, 4)), dma((8,)), dma((8,)), dma((8,)), dma((8,)),
        ],
        compiler_params=pltpu.CompilerParams(
            collective_id=1, has_side_effects=True, vmem_limit_bytes=VMEM_LIMIT
        ),
    )(M.reshape(2, UNITS, FEAT, TOK), G, up_count, down_count)


def solution(mesh):
    return jax.shard_map(
        shards,
        mesh=mesh,
        in_specs=(P("row", "col"),) * 10,
        out_specs=(P("row", "col"),) * 4,
        check_vma=False,
    )
```

```python
import jax
import jax.numpy as jnp
from jax import lax
from jax.experimental import pallas as pl
from jax.experimental.pallas import tpu as pltpu
from jax.sharding import PartitionSpec as P

BLK = 64
CAP = 4
TOK = 128
FEAT = 384
HALF = 192
HB = 24
NX, NY, NZ = 4, 4, 8
UNITS = 16
ROWS = 32
GELU_SCALE = 0.7978845608028654
GELU_CUBIC = 0.044715
MESH = pl.DeviceIdType.MESH
BF = jnp.bfloat16
F32 = jnp.float32
VMEM_LIMIT = 60 << 20
dma = pltpu.SemaphoreType.DMA
WTILE = (2, BLK, CAP * BLK)
UNIT = (2, HALF, TOK)
UF, UH, DF, DH = 0, 4, 8, 12


def coords():
    row, col = lax.axis_index("row"), lax.axis_index("col")
    return row % 4, col // 4, row // 4, (col // 2) % 2, col % 2


def dev(x, y, zl, zh, c):
    return (zl * 4 + x, y * 4 + zh * 2 + c)


def unit(y, zh, c):
    return y * 4 + zh * 2 + c


def remote(src, dst, ss, rs, to):
    return pltpu.make_async_remote_copy(
        src_ref=src, dst_ref=dst, send_sem=ss, recv_sem=rs, device_id=to, device_id_type=MESH
    )


def hello(x, y, zl, zh, c):
    barrier = pltpu.get_barrier_semaphore()

    def signal(to):
        pl.semaphore_signal(barrier, inc=1, device_id=to, device_id_type=MESH)

    for i in range(1, 4):
        signal(dev((x + i) % 4, y, zl, zh, c))
        signal(dev(x, (y + i) % 4, zl, zh, c))
    signal(dev(x, y, zl, 1 - zh, c))
    signal(dev(x, y, zl, zh, 1 - c))

    signal(dev(x, y, (zl + 1) % 8, jnp.where(zl == NZ - 1, 1 - zh, zh), c))
    signal(dev(x, y, (zl + 7) % 8, jnp.where(zl == 0, 1 - zh, zh), c))


def gelu_parts(v):
    t = jnp.tanh(GELU_SCALE * (v + GELU_CUBIC * v * v * v))
    values = 0.5 * v * (1.0 + t)
    slope = 0.5 * (1.0 + t) + 0.5 * v * (1.0 - t * t) * GELU_SCALE * (1.0 + 3.0 * GELU_CUBIC * v * v)
    return values, slope


def dot(a, b):
    return jnp.dot(a, b, preferred_element_type=F32)


def dot_nt(a, b):
    return lax.dot_general(a, b, (((1,), (1,)), ((), ())), preferred_element_type=F32)


def kernel(
    tok_h, grad_h, wup_h, wdn_h, uf_h, uh_h, uc_h, df_h, dh_h, dc_h,
    mixed, gin, gup, gdn,
    T0, T1, W, C, tok, grad, wup, wdn, uf, uh, uc, df, dh, dc, in_sem,
    t_send, t_recv, wz_send, wz_recv, wx_send, wx_recv, cz_send, cz_recv, cx_send, cx_recv,
    codes, table, order_v, order, p1, p2, run, act, slope, gp,
    M, G, rc, s1, ry, s2, rz, rx, sz, rl, rr, total,
    c_send, c_recv, y_sem_send, y_sem_recv, z_sem_send, z_sem_recv, x_send, x_recv,
    l_send, l_recv, r_send, r_recv,
):
    x, y, zl, zh, c = coords()
    T = (T0, T1)
    me, other = unit(y, zh, c), unit(y, 1 - zh, c)
    hbm = (tok_h, wup_h, wdn_h, uf_h, uh_h, uc_h, df_h, dh_h, dc_h, grad_h)
    local = (tok, wup, wdn, uf, uh, uc, df, dh, dc, grad)
    loads = [pltpu.make_async_copy(p, q, in_sem.at[n]) for n, (p, q) in enumerate(zip(hbm, local))]
    for cp in loads:
        cp.start()
    hello(x, y, zl, zh, c)

    def turn(a, ref):
        T[a][pl.ds(2 * me, 2)] = ref[...].astype(F32).T.astype(BF).reshape(2, 3, BLK, TOK)

    loads[0].wait()
    turn(0, tok)
    for cp in loads[1:9]:
        cp.wait()
    lane = lax.broadcasted_iota(jnp.int32, (1, 128), 1)
    code = jnp.zeros((1, 128), jnp.int32)
    for base, ref in ((0, uf), (4, uh), (8, df), (12, dh)):
        for s in range(CAP):
            code = jnp.where(lane == base + s, ref[0, s], code)
    C[x, zl] = code
    slot = lax.broadcasted_iota(jnp.int32, (BLK, CAP * BLK), 1) // BLK
    zero = jnp.zeros((BLK, CAP * BLK), F32)
    W[x, zl, 0] = jnp.where(slot < uc[0, 0], wup[...].astype(F32), zero).astype(BF)
    W[x, zl, 1] = jnp.where(slot < dc[0, 0], wdn[...].astype(F32), zero).astype(BF)
    loads[9].wait()
    turn(1, grad)
    pl.semaphore_wait(pltpu.get_barrier_semaphore(), 10)

    def chain(way, j, p):
        to = dev(x, y, zl + (1 if way == 0 else -1), zh, c)
        ref = W.at[x, j, p]
        return remote(ref, ref, wz_send.at[way, j, p], wz_recv.at[j, p], to)

    def code_chain(way, j):
        to = dev(x, y, zl + (1 if way == 0 else -1), zh, c)
        return remote(C.at[x, j], C.at[x, j], cz_send.at[way, j], cz_recv.at[j], to)

    def chain_start(way, j, p):
        @pl.when((zl < NZ - 1) if way == 0 else (zl > 0))
        def _():
            chain(way, j, p).start()
            if p == 0:
                code_chain(way, j).start()

    def spread(j, p, i):
        to = dev((x + i) % 4, y, zl, zh, c)
        ref = W.at[x, j, p]
        return remote(ref, ref, wx_send.at[j, i, p], wx_recv.at[x, j, p], to)

    def spread_start(j, p):
        for i in (1, 3, 2):
            spread(j, p, i).start()

    def t_copy(a, u, h, kind, to):
        ref = T[a].at[2 * u + h]
        return remote(ref, ref, t_send.at[a, h, kind], t_recv.at[a, 2 * u + h], to)

    def y_send(a, u, h, base):
        return [
            t_copy(a, u, h, base + n, dev(x, (y + i) % 4, zl, zh, c)) for n, i in enumerate((1, 3, 2))
        ]

    def core_send(a, u, h, n):
        return t_copy(a, u, h, 8 + n, dev(x, y, zl, zh, 1 - c))

    def z_send(a, h):
        return t_copy(a, me, h, 3, dev(x, y, zl, 1 - zh, c))

    def t_wait(a, u, h):
        t_copy(a, u, h, 7, dev(x, y, zl, zh, 1 - c)).wait_recv()

    def own(a):
        for h in range(2):
            for cp in y_send(a, me, h, 0):
                cp.start()
            core_send(a, me, h, 0).start()

    def near(a):
        for h in range(2):
            for n, i in enumerate((1, 3, 2)):
                u = unit((y + i) % 4, zh, c)
                t_wait(a, u, h)
                core_send(a, u, h, 2 + n).start()

    def partner(a, h):
        t_wait(a, other, h)
        for cp in y_send(a, other, h, 4):
            cp.start()
        core_send(a, other, h, 1).start()

    def far(a, h):
        for n, i in enumerate((1, 3, 2)):
            u = unit((y + i) % 4, 1 - zh, c)
            t_wait(a, u, h)
            core_send(a, u, h, 5 + n).start()

    def pull(t):
        for p in range(2):
            @pl.when(zl - t >= 0)
            def _():
                j = zl - t
                chain(0, j, p).wait_recv()
                if p == 0:
                    code_chain(0, j).wait_recv()
                chain_start(0, j, p)
                spread_start(j, p)

            @pl.when(zl + t <= NZ - 1)
            def _():
                j = zl + t
                chain(1, j, p).wait_recv()
                if p == 0:
                    code_chain(1, j).wait_recv()
                chain_start(1, j, p)
                spread_start(j, p)


    def xs(j, p, i):
        xt = (x + i) % 4
        return remote(
            G.at[xt, j, p], rx.at[i - 1, j, p], x_send.at[j, i, p], x_recv.at[j, i, p], dev(xt, y, zl, zh, c)
        )

    def cs(a, u):
        return remote(
            M.at[a, 2 * u + 1 - c], rc.at[a, u], c_send.at[a, u], c_recv.at[a, u], dev(x, y, zl, zh, 1 - c)
        )

    def ys(a, i, h):
        yt = (y + i) % 4
        return remote(
            s1.at[a, yt * 2 + h], ry.at[a, i - 1, h], y_sem_send.at[a, i - 1, h], y_sem_recv.at[a, i - 1, h],
            dev(x, yt, zl, zh, c),
        )

    def zs(a):
        return remote(s2.at[a], rz.at[a], z_sem_send.at[a], z_sem_recv.at[a], dev(x, y, zl, 1 - zh, c))

    def x_unit(j, p):
        for i in (1, 3, 2):
            xs(j, p, i).start()

    def add_core(a, u):
        cs(a, u).wait_recv()
        s1[a, u] = (M[a, 2 * u + c].astype(F32) + rc[a, u].astype(F32)).astype(BF)

    def core_stage(a):
        for h in (0, 1):
            hh = jnp.where(h == 0, 1 - zh, zh)
            for i in (1, 3, 2):
                add_core(a, ((y + i) % 4) * 2 + hh)
                ys(a, i, hh).start()
        for h in range(2):
            add_core(a, y * 2 + h)

    def y_sum(a, h):
        for i in range(1, 4):
            ys(a, i, h).wait_recv()
        acc = s1[a, y * 2 + h].astype(F32)
        for i in range(3):
            acc = acc + ry[a, i, h].astype(F32)
        return acc

    def y_stage(a):
        s2[a] = y_sum(a, 1 - zh).astype(BF)
        zs(a).start()

    def z_stage(a, out):
        own = y_sum(a, zh)
        zs(a).wait_recv()
        out[...] = (own + rz[a].astype(F32)).reshape(FEAT, TOK).T.astype(BF)

    def x_sum(j, p):
        for i in range(1, 4):
            xs(j, p, i).wait_recv()
        acc = G[x, j, p].astype(F32)
        for i in range(3):
            acc = acc + rx[i, j, p].astype(F32)
        return acc

    def left(j, p):
        to = dev(x, y, zl - 1, zh, c)
        return remote(sz.at[j, p], rl.at[j, p], l_send.at[j, p], l_recv.at[j, p], to)

    def right(j, p):
        to = dev(x, y, zl + 1, zh, c)
        return remote(sz.at[j, p], rr.at[j, p], r_send.at[j, p], r_recv.at[j, p], to)

    def pass_on(j, p, move, got, first):
        acc = x_sum(j, p)

        @pl.when(first)
        def _():
            sz[j, p] = acc.astype(BF)

        @pl.when(jnp.logical_not(first))
        def _():
            move(j, p).wait_recv()
            sz[j, p] = (acc + got[j, p].astype(F32)).astype(BF)

        move(j, p).start()

    def step(t, p):
        @pl.when(t >= NZ - 1 - zl)
        def _():
            pass_on(t - NZ + 1 + zl, p, left, rl, zl == NZ - 1)

        @pl.when(t >= zl)
        def _():
            pass_on(NZ - 1 - t + zl, p, right, rr, zl == 0)


    def code(r, k):
        return codes[r % 4, r // 4, 0, k]

    def forward(j, xx):
        r = j * 4 + xx
        wt = W[xx, j, 0].astype(F32).T.astype(BF)
        for s in range(CAP):
            p1[r * CAP + s] = dot(wt[s * BLK : (s + 1) * BLK], T[0][r, code(r, UF + s)])

    def backward(j, xx):
        r = j * 4 + xx
        w = W[xx, j, 1]
        for s in range(CAP):
            p2[r * CAP + s] = dot(w[:, s * BLK : (s + 1) * BLK], T[1][r, code(r, DF + s)])

    def slot_masks(r, base):
        lane = lax.broadcasted_iota(jnp.int32, (1, CAP * BLK), 1) // BLK
        which = jnp.zeros((1, CAP * BLK), jnp.int32)
        for s in range(CAP):
            which = jnp.where(lane == s, code(r, base + s), which)
        return [jnp.where(which == f, 1.0, 0.0).astype(BF) for f in range(3)]

    def mixed_tile(r):
        w = W[r % 4, r // 4, 1].astype(F32)
        w = jnp.concatenate([w[:, s * BLK : (s + 1) * BLK].T for s in range(CAP)], axis=1).astype(BF)
        lhs = jnp.concatenate([w * m for m in slot_masks(r, DF)], axis=0)
        rhs = jnp.concatenate([act[code(r, DH + s)] for s in range(CAP)], axis=0)
        M[0, r // 2, r % 2] = dot(lhs, rhs).astype(BF)

    def input_tile(r):
        w = W[r % 4, r // 4, 0]
        lhs = jnp.concatenate([w * m for m in slot_masks(r, UF)], axis=0)
        rhs = jnp.concatenate([gp[code(r, UH + s)] for s in range(CAP)], axis=0)
        M[1, r // 2, r % 2] = dot(lhs, rhs).astype(BF)

    def down_tile(j, xx):
        r = j * 4 + xx
        parts = [dot_nt(act[code(r, DH + s)], T[1][r, code(r, DF + s)]) for s in range(CAP)]
        G[xx, j, 1] = jnp.concatenate(parts, axis=1).astype(BF)

    def up_tile(j, xx):
        r = j * 4 + xx
        parts = [dot_nt(T[0][r, code(r, UF + s)], gp[code(r, UH + s)]) for s in range(CAP)]
        G[xx, j, 0] = jnp.concatenate(parts, axis=1).astype(BF)

    def sort_slots(base, row):
        col_at = lax.broadcasted_iota(jnp.int32, (ROWS, 1), 0)
        lane128 = lax.broadcasted_iota(jnp.int32, (ROWS, 128), 1)
        keys = table[0:ROWS, :]
        turned = table[...].T
        perm = jnp.zeros((1, 128), jnp.int32)
        sorted_keys = jnp.zeros((1, 128), jnp.int32)
        below = jnp.zeros((1, 128), jnp.int32)
        for s in range(CAP):
            mine = jnp.sum(jnp.where(lane128 == base + s, keys, 0), axis=1, keepdims=True)
            rank = jnp.zeros((ROWS, 1), jnp.int32)
            for o in range(CAP):
                theirs = turned[base + o : base + o + 1, :]
                first = (theirs < mine) | ((theirs == mine) & (o * ROWS + lane128 < s * ROWS + col_at))
                first = first & (lane128 < ROWS)
                rank = rank + jnp.sum(jnp.where(first, 1, 0), axis=1, keepdims=True)
            here = rank == lane128
            perm = perm + jnp.sum(jnp.where(here, col_at * CAP + s, 0), axis=0, keepdims=True)
            sorted_keys = sorted_keys + jnp.sum(jnp.where(here, mine, 0), axis=0, keepdims=True)
            below = below + jnp.sum(jnp.where(mine < lane128, 1, 0), axis=0, keepdims=True)
        order_v[row : row + 1] = perm
        order_v[row + 1 : row + 2] = sorted_keys
        order_v[row + 2 : row + 3] = below

    def segment_sums(src, row):
        def add(i, carry):
            keep = order[row + 1, i] == order[row + 1, jnp.maximum(i - 1, 0)]
            carry = jnp.where(keep, carry, 0.0) + src[order[row, i]]
            run[i + 1] = carry
            return carry

        lax.fori_loop(0, ROWS * CAP, add, jnp.zeros((BLK, TOK), F32), unroll=4)

    def segment(row, k):
        last = order[row + 2, k + 1]
        return jnp.where(last > order[row + 2, k], run[last], 0.0)

    def tiles(fn):
        @pl.loop(0, NZ)
        def _(j):
            for xx in range(NX):
                fn(j, xx)

    def units(fn, a, mine):
        @pl.loop(0, 8)
        def _(v):
            u = 2 * v + (c if mine else 1 - c)
            for h in range(2):
                fn(2 * u + h)
            if not mine:
                cs(a, v).start()

    def wave(fn, p):
        def one(j):
            for xx in range(NX):
                fn(j, xx)
            x_unit(j, p)

        @pl.loop(0, NZ - 1)
        def _(t):
            @pl.when(t >= NZ - 1 - zl)
            def _():
                one(t - NZ + 1 + zl)

            @pl.when(t >= zl)
            def _():
                one(NZ - 1 - t + zl)

        one(zl)
    for p in range(2):
        chain_start(0, zl, p)
        chain_start(1, zl, p)
        if p == 0:
            z_send(0, 0).start()
        spread_start(zl, p)
    own(0)
    z_send(0, 1).start()
    own(1)

    pull(1)
    pull(2)
    near(0)
    pull(3)
    z_send(1, 0).start()
    partner(0, 0)
    pull(4)
    partner(0, 1)
    near(1)
    z_send(1, 1).start()
    pull(5)
    far(0, 0)
    pull(6)
    far(0, 1)
    pull(7)

    def code_send(i):
        to = dev((x + i) % 4, y, zl, zh, c)
        return remote(C.at[x], C.at[x], cx_send.at[i], cx_recv.at[x], to)

    for i in range(1, 4):
        code_send(i).start()
    partner(1, 0)
    for i in range(1, 4):
        xs_ = (x + i) % 4
        to = dev(xs_, y, zl, zh, c)
        remote(C.at[xs_], C.at[xs_], cx_send.at[i], cx_recv.at[xs_], to).wait_recv()
    to_smem = pltpu.make_async_copy(C, codes, in_sem.at[0])
    to_smem.start()
    table[...] = jnp.zeros_like(table)
    order_v[...] = jnp.zeros_like(order_v)
    run[0] = jnp.zeros((BLK, TOK), F32)
    for r in range(ROWS):
        table[r : r + 1] = C[r % 4, r // 4]
    sort_slots(UH, 0)
    sort_slots(DH, 3)
    order_copy = pltpu.make_async_copy(order_v, order, in_sem.at[1])
    order_copy.start()
    for i in range(1, 4):
        xs_ = (x + i) % 4
        to = dev(xs_, y, zl, zh, c)

        @pl.loop(0, NZ)
        def _(j):
            for p in range(2):
                ref = W.at[xs_, j, p]
                remote(ref, ref, wx_send.at[j, i, p], wx_recv.at[xs_, j, p], to).wait_recv()

    def core_wait(a):
        @pl.loop(0, 8)
        def _(v):
            for h in range(2):
                t_wait(a, 2 * v + 1 - c, h)

    core_wait(0)
    to_smem.wait()
    order_copy.wait()
    tiles(forward)
    partner(1, 1)
    far(1, 0)
    segment_sums(p1, 0)

    @pl.loop(0, HB)
    def _(k):
        v, d = gelu_parts(segment(0, k))
        act[k] = v.astype(BF)
        slope[k] = d

    far(1, 1)
    units(mixed_tile, 0, False)
    units(mixed_tile, 0, True)
    core_wait(1)
    tiles(backward)
    core_stage(0)
    segment_sums(p2, 3)

    @pl.loop(0, HB)
    def _(k):
        gp[k] = (segment(3, k) * slope[k]).astype(BF)

    wave(up_tile, 0)
    y_stage(0)
    step(0, 0)
    wave(down_tile, 1)
    step(1, 0)
    units(input_tile, 1, False)
    step(2, 0)
    units(input_tile, 1, True)
    step(3, 0)
    step(0, 1)
    core_stage(1)
    step(4, 0)
    step(1, 1)
    step(5, 0)
    step(2, 1)
    y_stage(1)
    step(6, 0)
    for t in range(3, 7):
        step(t, 1)
    owns = []
    for p in range(2):
        total[...] = x_sum(zl, p)

        @pl.when(zl < NZ - 1)
        def _():
            left(zl, p).wait_recv()
            total[...] += rl[zl, p].astype(F32)

        @pl.when(zl > 0)
        def _():
            right(zl, p).wait_recv()
            total[...] += rr[zl, p].astype(F32)

        owns.append(total[...])
    slot = lax.broadcasted_iota(jnp.int32, (BLK, CAP * BLK), 1) // BLK
    gup[...] = jnp.where(slot < uc[0, 0], owns[0], 0.0).astype(BF)
    gdn[...] = jnp.where(slot < dc[0, 0], owns[1], 0.0).astype(BF)
    z_stage(0, mixed)
    z_stage(1, gin)

    for i in range(1, 4):
        code_send(i).wait_send()

        @pl.loop(0, NZ)
        def _(j):
            for p in range(2):
                spread(j, p, i).wait_send()

    @pl.loop(0, NZ)
    def _(j):
        @pl.when((j <= zl) & (zl < NZ - 1))
        def _():
            code_chain(0, j).wait_send()
            for p in range(2):
                chain(0, j, p).wait_send()

        @pl.when((j >= zl) & (zl > 0))
        def _():
            code_chain(1, j).wait_send()
            for p in range(2):
                chain(1, j, p).wait_send()

    for a in range(2):
        for h in range(2):
            z_send(a, h).wait_send()
            for u, base in ((me, 0), (other, 4)):
                for cp in y_send(a, u, h, base):
                    cp.wait_send()
            for n in range(8):
                core_send(a, me, h, n).wait_send()

    for a in range(2):
        zs(a).wait_send()
        for u in range(8):
            cs(a, u).wait_send()
        for i in range(1, 4):
            for h in range(2):
                ys(a, i, h).wait_send()

    @pl.loop(0, NZ)
    def _(j):
        for p in range(2):
            for i in range(1, 4):
                xs(j, p, i).wait_send()

        @pl.when(j < zl)
        def _():
            for p in range(2):
                left(j, p).wait_send()

        @pl.when(j > zl)
        def _():
            for p in range(2):
                right(j, p).wait_send()


def vmem():
    return pl.BlockSpec(memory_space=pltpu.VMEM)


def shards(tokens, w_up, up_feat, up_hid, up_count, w_down, down_feat, down_hid, down_count, grad_out):
    V, S, I32 = pltpu.VMEM, pltpu.SMEM, jnp.int32
    scratch = [
        V((ROWS, 3, BLK, TOK), BF), V((ROWS, 3, BLK, TOK), BF), V((NX, NZ) + WTILE, BF), V((NX, NZ, 1, 128), I32),
        V((TOK, FEAT), BF), V((TOK, FEAT), BF), V((BLK, CAP * BLK), BF), V((BLK, CAP * BLK), BF),
        S((1, CAP), I32), S((1, CAP), I32), S((1, 1), I32), S((1, CAP), I32), S((1, CAP), I32), S((1, 1), I32),
        dma((10,)),
        dma((2, 2, 16)), dma((2, ROWS)), dma((2, NZ, 2)), dma((NZ, 2)), dma((NZ, 4, 2)), dma((NX, NZ, 2)),
        dma((2, NZ)), dma((NZ,)), dma((4,)), dma((4,)),
        S((NX, NZ, 1, 128), I32), V((128, 128), I32), V((8, 128), I32), S((8, 128), I32),
        V((ROWS * CAP, BLK, TOK), F32), V((ROWS * CAP, BLK, TOK), F32), V((ROWS * CAP + 1, BLK, TOK), F32),
        V((HB, BLK, TOK), BF), V((HB, BLK, TOK), F32), V((HB, BLK, TOK), BF),
        V((2, UNITS) + UNIT, BF), V((NX, NZ) + WTILE, BF),
        V((2, 8) + UNIT, BF), V((2, 8) + UNIT, BF), V((2, 3, 2) + UNIT, BF), V((2,) + UNIT, BF), V((2,) + UNIT, BF),
        V((3, NZ) + WTILE, BF), V((NZ,) + WTILE, BF), V((NZ,) + WTILE, BF), V((NZ,) + WTILE, BF),
        V((BLK, CAP * BLK), F32),
        dma((2, 8)), dma((2, 8)), dma((2, 3, 2)), dma((2, 3, 2)), dma((2,)), dma((2,)),
        dma((8, 4, 2)), dma((8, 4, 2)), dma((8, 2)), dma((8, 2)), dma((8, 2)), dma((8, 2)),
    ]
    return pl.pallas_call(
        kernel,
        name="ffn",
        out_shape=(
            jax.ShapeDtypeStruct((TOK, FEAT), BF),
            jax.ShapeDtypeStruct((TOK, FEAT), BF),
            jax.ShapeDtypeStruct((BLK, CAP * BLK), BF),
            jax.ShapeDtypeStruct((BLK, CAP * BLK), BF),
        ),
        in_specs=[pl.BlockSpec(memory_space=pltpu.HBM)] * 10,
        out_specs=(vmem(),) * 4,
        scratch_shapes=scratch,
        compiler_params=pltpu.CompilerParams(
            collective_id=0, has_side_effects=True, vmem_limit_bytes=VMEM_LIMIT
        ),
    )(tokens, grad_out, w_up, w_down, up_feat, up_hid, up_count, down_feat, down_hid, down_count)


def solution(mesh):
    return jax.shard_map(
        shards,
        mesh=mesh,
        in_specs=(P("row", "col"),) * 10,
        out_specs=(P("row", "col"),) * 4,
        check_vma=False,
    )
```

```python
import jax
import jax.numpy as jnp
from jax import lax
from jax.experimental import pallas as pl
from jax.experimental.pallas import tpu as pltpu
from jax.sharding import PartitionSpec as P

BLK = 64
CAP = 4
TOK = 128
FEAT = 384
HALF = 192
HB = 24
NX, NY, NZ = 4, 4, 8
UNITS = 16
ROWS = 32
GELU_SCALE = 0.7978845608028654
GELU_CUBIC = 0.044715
MESH = pl.DeviceIdType.MESH
BF = jnp.bfloat16
F32 = jnp.float32
VMEM_LIMIT = 60 << 20
dma = pltpu.SemaphoreType.DMA
WTILE = (2, BLK, CAP * BLK)
UNIT = (2, HALF, TOK)
UF, UH, DF, DH = 0, 4, 8, 12


def coords():
    row, col = lax.axis_index("row"), lax.axis_index("col")
    return row % 4, col // 4, row // 4, (col // 2) % 2, col % 2


def dev(x, y, zl, zh, c):
    return (zl * 4 + x, y * 4 + zh * 2 + c)


def unit(y, zh, c):
    return y * 4 + zh * 2 + c


def remote(src, dst, ss, rs, to):
    return pltpu.make_async_remote_copy(
        src_ref=src, dst_ref=dst, send_sem=ss, recv_sem=rs, device_id=to, device_id_type=MESH
    )


def hello(x, y, zl, zh, c):
    barrier = pltpu.get_barrier_semaphore()

    def signal(to):
        pl.semaphore_signal(barrier, inc=1, device_id=to, device_id_type=MESH)

    for i in range(1, 4):
        signal(dev((x + i) % 4, y, zl, zh, c))
        signal(dev(x, (y + i) % 4, zl, zh, c))
    signal(dev(x, y, zl, 1 - zh, c))
    signal(dev(x, y, zl, zh, 1 - c))

    signal(dev(x, y, (zl + 1) % 8, jnp.where(zl == NZ - 1, 1 - zh, zh), c))
    signal(dev(x, y, (zl + 7) % 8, jnp.where(zl == 0, 1 - zh, zh), c))


def gelu_parts(v):
    t = jnp.tanh(GELU_SCALE * (v + GELU_CUBIC * v * v * v))
    values = 0.5 * v * (1.0 + t)
    slope = 0.5 * (1.0 + t) + 0.5 * v * (1.0 - t * t) * GELU_SCALE * (1.0 + 3.0 * GELU_CUBIC * v * v)
    return values, slope


def dot(a, b):
    return jnp.dot(a, b, preferred_element_type=F32)


def dot_nt(a, b):
    return lax.dot_general(a, b, (((1,), (1,)), ((), ())), preferred_element_type=F32)


def kernel(
    tok_h, grad_h, wup_h, wdn_h, uf_h, uh_h, uc_h, df_h, dh_h, dc_h,
    mixed, gin, gup, gdn,
    T0, T1, W, C, tok, grad, wup, wdn, uf, uh, uc, df, dh, dc, in_sem,
    t_send, t_recv, wz_send, wz_recv, wx_send, wx_recv, cz_send, cz_recv, cx_send, cx_recv,
    codes, table, order_v, order, p1, p2, run, act, slope, gp,
    lhs, M, G, rc, s1, ry, s2, rz, rx, sz, rl, rr, total,
    c_send, c_recv, y_sem_send, y_sem_recv, z_sem_send, z_sem_recv, x_send, x_recv,
    l_send, l_recv, r_send, r_recv,
):
    x, y, zl, zh, c = coords()
    T = (T0, T1)
    me, other = unit(y, zh, c), unit(y, 1 - zh, c)
    hbm = (tok_h, wup_h, wdn_h, uf_h, uh_h, uc_h, df_h, dh_h, dc_h, grad_h)
    local = (tok, wup, wdn, uf, uh, uc, df, dh, dc, grad)
    loads = [pltpu.make_async_copy(p, q, in_sem.at[n]) for n, (p, q) in enumerate(zip(hbm, local))]
    for cp in loads:
        cp.start()
    hello(x, y, zl, zh, c)

    def turn(a, ref):
        T[a][pl.ds(2 * me, 2)] = ref[...].astype(F32).T.astype(BF).reshape(2, 3, BLK, TOK)

    loads[0].wait()
    turn(0, tok)
    for cp in loads[1:9]:
        cp.wait()
    lane = lax.broadcasted_iota(jnp.int32, (1, 128), 1)
    code = jnp.zeros((1, 128), jnp.int32)
    for base, ref in ((0, uf), (4, uh), (8, df), (12, dh)):
        for s in range(CAP):
            code = jnp.where(lane == base + s, ref[0, s], code)
    C[x, zl] = code
    slot = lax.broadcasted_iota(jnp.int32, (BLK, CAP * BLK), 1) // BLK
    zero = jnp.zeros((BLK, CAP * BLK), F32)
    W[x, zl, 0] = jnp.where(slot < uc[0, 0], wup[...].astype(F32), zero).astype(BF)
    W[x, zl, 1] = jnp.where(slot < dc[0, 0], wdn[...].astype(F32), zero).astype(BF)
    loads[9].wait()
    turn(1, grad)
    pl.semaphore_wait(pltpu.get_barrier_semaphore(), 10)

    def chain(way, j, p):
        to = dev(x, y, zl + (1 if way == 0 else -1), zh, c)
        ref = W.at[x, j, p]
        return remote(ref, ref, wz_send.at[way, j, p], wz_recv.at[j, p], to)

    def code_chain(way, j):
        to = dev(x, y, zl + (1 if way == 0 else -1), zh, c)
        return remote(C.at[x, j], C.at[x, j], cz_send.at[way, j], cz_recv.at[j], to)

    def chain_start(way, j, p):
        @pl.when((zl < NZ - 1) if way == 0 else (zl > 0))
        def _():
            chain(way, j, p).start()
            if p == 0:
                code_chain(way, j).start()

    def spread(j, p, i):
        to = dev((x + i) % 4, y, zl, zh, c)
        ref = W.at[x, j, p]
        return remote(ref, ref, wx_send.at[j, i, p], wx_recv.at[x, j, p], to)

    def spread_start(j, p):
        for i in (1, 3, 2):
            spread(j, p, i).start()

    def t_copy(a, u, h, kind, to):
        ref = T[a].at[2 * u + h]
        return remote(ref, ref, t_send.at[a, h, kind], t_recv.at[a, 2 * u + h], to)

    def y_send(a, u, h, base):
        return [
            t_copy(a, u, h, base + n, dev(x, (y + i) % 4, zl, zh, c)) for n, i in enumerate((1, 3, 2))
        ]

    def core_send(a, u, h, n):
        return t_copy(a, u, h, 8 + n, dev(x, y, zl, zh, 1 - c))

    def z_send(a, h):
        return t_copy(a, me, h, 3, dev(x, y, zl, 1 - zh, c))

    def t_wait(a, u, h):
        t_copy(a, u, h, 7, dev(x, y, zl, zh, 1 - c)).wait_recv()

    def own(a):
        for h in range(2):
            for cp in y_send(a, me, h, 0):
                cp.start()
            core_send(a, me, h, 0).start()

    def near(a):
        for h in range(2):
            for n, i in enumerate((1, 3, 2)):
                u = unit((y + i) % 4, zh, c)
                t_wait(a, u, h)
                core_send(a, u, h, 2 + n).start()

    def partner(a, h):
        t_wait(a, other, h)
        for cp in y_send(a, other, h, 4):
            cp.start()
        core_send(a, other, h, 1).start()

    def far(a, h):
        for n, i in enumerate((1, 3, 2)):
            u = unit((y + i) % 4, 1 - zh, c)
            t_wait(a, u, h)
            core_send(a, u, h, 5 + n).start()

    def pull(t):
        for p in range(2):
            @pl.when(zl - t >= 0)
            def _():
                j = zl - t
                chain(0, j, p).wait_recv()
                if p == 0:
                    code_chain(0, j).wait_recv()
                chain_start(0, j, p)
                spread_start(j, p)

            @pl.when(zl + t <= NZ - 1)
            def _():
                j = zl + t
                chain(1, j, p).wait_recv()
                if p == 0:
                    code_chain(1, j).wait_recv()
                chain_start(1, j, p)
                spread_start(j, p)


    def xs(j, p, i):
        xt = (x + i) % 4
        return remote(
            G.at[xt, j, p], rx.at[i - 1, j, p], x_send.at[j, i, p], x_recv.at[j, i, p], dev(xt, y, zl, zh, c)
        )

    def cs(a, u):
        return remote(
            M.at[a, 2 * u + 1 - c], rc.at[a, u], c_send.at[a, u], c_recv.at[a, u], dev(x, y, zl, zh, 1 - c)
        )

    def ys(a, i, h):
        yt = (y + i) % 4
        return remote(
            s1.at[a, yt * 2 + h], ry.at[a, i - 1, h], y_sem_send.at[a, i - 1, h], y_sem_recv.at[a, i - 1, h],
            dev(x, yt, zl, zh, c),
        )

    def zs(a):
        return remote(s2.at[a], rz.at[a], z_sem_send.at[a], z_sem_recv.at[a], dev(x, y, zl, 1 - zh, c))

    def x_unit(j, p):
        for i in (1, 3, 2):
            xs(j, p, i).start()

    def add_core(a, u):
        cs(a, u).wait_recv()
        s1[a, u] = (M[a, 2 * u + c].astype(F32) + rc[a, u].astype(F32)).astype(BF)

    def core_stage(a):
        for h in (0, 1):
            hh = jnp.where(h == 0, 1 - zh, zh)
            for i in (1, 3, 2):
                add_core(a, ((y + i) % 4) * 2 + hh)
                ys(a, i, hh).start()
        for h in range(2):
            add_core(a, y * 2 + h)

    def y_sum(a, h):
        for i in range(1, 4):
            ys(a, i, h).wait_recv()
        acc = s1[a, y * 2 + h].astype(F32)
        for i in range(3):
            acc = acc + ry[a, i, h].astype(F32)
        return acc

    def y_stage(a):
        s2[a] = y_sum(a, 1 - zh).astype(BF)
        zs(a).start()

    def z_stage(a, out):
        own = y_sum(a, zh)
        zs(a).wait_recv()
        out[...] = (own + rz[a].astype(F32)).reshape(FEAT, TOK).T.astype(BF)

    def x_sum(j, p):
        for i in range(1, 4):
            xs(j, p, i).wait_recv()
        acc = G[x, j, p].astype(F32)
        for i in range(3):
            acc = acc + rx[i, j, p].astype(F32)
        return acc

    def left(j, p):
        to = dev(x, y, zl - 1, zh, c)
        return remote(sz.at[j, p], rl.at[j, p], l_send.at[j, p], l_recv.at[j, p], to)

    def right(j, p):
        to = dev(x, y, zl + 1, zh, c)
        return remote(sz.at[j, p], rr.at[j, p], r_send.at[j, p], r_recv.at[j, p], to)

    def pass_on(j, p, move, got, first):
        acc = x_sum(j, p)

        @pl.when(first)
        def _():
            sz[j, p] = acc.astype(BF)

        @pl.when(jnp.logical_not(first))
        def _():
            move(j, p).wait_recv()
            sz[j, p] = (acc + got[j, p].astype(F32)).astype(BF)

        move(j, p).start()

    def step(t, p):
        @pl.when(t >= NZ - 1 - zl)
        def _():
            pass_on(t - NZ + 1 + zl, p, left, rl, zl == NZ - 1)

        @pl.when(t >= zl)
        def _():
            pass_on(NZ - 1 - t + zl, p, right, rr, zl == 0)


    def code(r, k):
        return codes[r % 4, r // 4, 0, k]

    def forward(j, xx):
        r = j * 4 + xx
        wt = W[xx, j, 0].astype(F32).T.astype(BF)
        for s in range(CAP):
            p1[r * CAP + s] = dot(wt[s * BLK : (s + 1) * BLK], T[0][r, code(r, UF + s)])

    def backward(j, xx):
        r = j * 4 + xx
        w = W[xx, j, 1]
        for s in range(CAP):
            p2[r * CAP + s] = dot(w[:, s * BLK : (s + 1) * BLK], T[1][r, code(r, DF + s)])

    def slot_masks(r, base):
        lane = lax.broadcasted_iota(jnp.int32, (1, CAP * BLK), 1) // BLK
        which = jnp.zeros((1, CAP * BLK), jnp.int32)
        for s in range(CAP):
            which = jnp.where(lane == s, code(r, base + s), which)
        return [jnp.where(which == f, 1.0, 0.0).astype(BF) for f in range(3)]

    def expand(r):
        w = W[r % 4, r // 4, 0]
        lhs[1, r] = jnp.concatenate([w * m for m in slot_masks(r, UF)], axis=0)
        w = W[r % 4, r // 4, 1].astype(F32)
        w = jnp.concatenate([w[:, s * BLK : (s + 1) * BLK].T for s in range(CAP)], axis=1).astype(BF)
        lhs[0, r] = jnp.concatenate([w * m for m in slot_masks(r, DF)], axis=0)

    def mixed_tile(r):
        rhs = jnp.concatenate([act[code(r, DH + s)] for s in range(CAP)], axis=0)
        M[0, r // 2, r % 2] = dot(lhs[0, r], rhs).astype(BF)

    def input_tile(r):
        rhs = jnp.concatenate([gp[code(r, UH + s)] for s in range(CAP)], axis=0)
        M[1, r // 2, r % 2] = dot(lhs[1, r], rhs).astype(BF)

    def expand_all():
        @pl.loop(0, ROWS, unroll=2)
        def _(r):
            expand(r)

    def down_tile(j, xx):
        r = j * 4 + xx
        parts = [dot_nt(act[code(r, DH + s)], T[1][r, code(r, DF + s)]) for s in range(CAP)]
        G[xx, j, 1] = jnp.concatenate(parts, axis=1).astype(BF)

    def up_tile(j, xx):
        r = j * 4 + xx
        parts = [dot_nt(T[0][r, code(r, UF + s)], gp[code(r, UH + s)]) for s in range(CAP)]
        G[xx, j, 0] = jnp.concatenate(parts, axis=1).astype(BF)

    def sort_slots(base, row):
        col_at = lax.broadcasted_iota(jnp.int32, (ROWS, 1), 0)
        lane128 = lax.broadcasted_iota(jnp.int32, (ROWS, 128), 1)
        keys = table[0:ROWS, :]
        turned = table[...].T
        perm = jnp.zeros((1, 128), jnp.int32)
        sorted_keys = jnp.zeros((1, 128), jnp.int32)
        below = jnp.zeros((1, 128), jnp.int32)
        for s in range(CAP):
            mine = jnp.sum(jnp.where(lane128 == base + s, keys, 0), axis=1, keepdims=True)
            rank = jnp.zeros((ROWS, 1), jnp.int32)
            for o in range(CAP):
                theirs = turned[base + o : base + o + 1, :]
                first = (theirs < mine) | ((theirs == mine) & (o * ROWS + lane128 < s * ROWS + col_at))
                first = first & (lane128 < ROWS)
                rank = rank + jnp.sum(jnp.where(first, 1, 0), axis=1, keepdims=True)
            here = rank == lane128
            perm = perm + jnp.sum(jnp.where(here, col_at * CAP + s, 0), axis=0, keepdims=True)
            sorted_keys = sorted_keys + jnp.sum(jnp.where(here, mine, 0), axis=0, keepdims=True)
            below = below + jnp.sum(jnp.where(mine < lane128, 1, 0), axis=0, keepdims=True)
        order_v[row : row + 1] = perm
        order_v[row + 1 : row + 2] = sorted_keys
        order_v[row + 2 : row + 3] = below

    def segment_sums(src, row):
        def add(i, carry):
            keep = order[row + 1, i] == order[row + 1, jnp.maximum(i - 1, 0)]
            carry = jnp.where(keep, carry, 0.0) + src[order[row, i]]
            run[i + 1] = carry
            return carry

        lax.fori_loop(0, ROWS * CAP, add, jnp.zeros((BLK, TOK), F32), unroll=4)

    def segment(row, k):
        last = order[row + 2, k + 1]
        return jnp.where(last > order[row + 2, k], run[last], 0.0)

    def tiles(fn, start=0, end=NZ):
        @pl.loop(start, end)
        def _(j):
            for xx in range(NX):
                fn(j, xx)

    def units(fn, a, mine):
        @pl.loop(0, 8)
        def _(n):
            v = 2 * (n % 4) + jnp.where(n < 4, 1 - zh, zh)
            u = 2 * v + (c if mine else 1 - c)
            for h in range(2):
                fn(2 * u + h)
            if not mine:
                cs(a, v).start()

    def wave(fn, p):
        def one(j):
            for xx in range(NX):
                fn(j, xx)
            x_unit(j, p)

        @pl.loop(0, NZ - 1)
        def _(t):
            @pl.when(t >= NZ - 1 - zl)
            def _():
                one(t - NZ + 1 + zl)

            @pl.when(t >= zl)
            def _():
                one(NZ - 1 - t + zl)

        one(zl)
    for p in range(2):
        chain_start(0, zl, p)
        chain_start(1, zl, p)
        if p == 0:
            z_send(0, 0).start()
        spread_start(zl, p)
    def code_send(i):
        to = dev((x + i) % 4, y, zl, zh, c)
        return remote(C.at[x], C.at[x], cx_send.at[i], cx_recv.at[x], to)

    def code_sends():
        for i in range(1, 4):
            code_send(i).start()

    to_smem = pltpu.make_async_copy(C, codes, in_sem.at[0])
    order_copy = pltpu.make_async_copy(order_v, order, in_sem.at[1])

    def settle():
        for i in range(1, 4):
            xt = (x + i) % 4
            to = dev(xt, y, zl, zh, c)
            remote(C.at[xt], C.at[xt], cx_send.at[i], cx_recv.at[xt], to).wait_recv()
        to_smem.start()
        table[...] = jnp.zeros_like(table)
        order_v[...] = jnp.zeros_like(order_v)
        run[0] = jnp.zeros((BLK, TOK), F32)
        for r in range(ROWS):
            table[r : r + 1] = C[r % 4, r // 4]
        sort_slots(UH, 0)
        sort_slots(DH, 3)
        order_copy.start()
        for i in range(1, 4):
            xt = (x + i) % 4
            to = dev(xt, y, zl, zh, c)

            @pl.loop(0, NZ)
            def _(j):
                for p in range(2):
                    ref = W.at[xt, j, p]
                    remote(ref, ref, wx_send.at[j, i, p], wx_recv.at[xt, j, p], to).wait_recv()

        to_smem.wait()
        order_copy.wait()

    def core_wait(a):
        @pl.loop(0, 8)
        def _(v):
            for h in range(2):
                t_wait(a, 2 * v + 1 - c, h)

    def gelu():
        @pl.loop(0, HB)
        def _(k):
            v, d = gelu_parts(segment(0, k))
            act[k] = v.astype(BF)
            slope[k] = d

    def grad_pre():
        @pl.loop(0, HB)
        def _(k):
            gp[k] = (segment(3, k) * slope[k]).astype(BF)

    own(0)
    z_send(0, 1).start()
    own(1)
    pull(1)
    pull(2)
    near(0)
    pull(3)
    z_send(1, 0).start()
    partner(0, 0)
    pull(4)
    z_send(1, 1).start()
    partner(0, 1)
    near(1)
    pull(5)
    far(0, 0)
    pull(6)
    far(0, 1)
    partner(1, 0)
    pull(7)
    code_sends()
    partner(1, 1)
    settle()
    core_wait(0)
    expand_all()
    tiles(forward)
    far(1, 0)
    far(1, 1)
    segment_sums(p1, 0)
    gelu()
    units(mixed_tile, 0, False)
    units(mixed_tile, 0, True)
    core_wait(1)
    wave(down_tile, 1)
    core_stage(0)
    tiles(backward)
    step(0, 1)
    segment_sums(p2, 3)
    grad_pre()
    step(1, 1)
    wave(up_tile, 0)
    step(0, 0)
    y_stage(0)
    step(2, 1)
    units(input_tile, 1, False)
    step(1, 0)
    step(3, 1)
    units(input_tile, 1, True)
    step(2, 0)
    step(4, 1)
    core_stage(1)
    step(3, 0)
    step(5, 1)
    step(4, 0)
    step(6, 1)
    y_stage(1)
    step(5, 0)
    step(6, 0)
    owns = []
    for p in range(2):
        total[...] = x_sum(zl, p)

        @pl.when(zl < NZ - 1)
        def _():
            left(zl, p).wait_recv()
            total[...] += rl[zl, p].astype(F32)

        @pl.when(zl > 0)
        def _():
            right(zl, p).wait_recv()
            total[...] += rr[zl, p].astype(F32)

        owns.append(total[...])
    slot = lax.broadcasted_iota(jnp.int32, (BLK, CAP * BLK), 1) // BLK
    gup[...] = jnp.where(slot < uc[0, 0], owns[0], 0.0).astype(BF)
    gdn[...] = jnp.where(slot < dc[0, 0], owns[1], 0.0).astype(BF)
    z_stage(0, mixed)
    z_stage(1, gin)

    for i in range(1, 4):
        code_send(i).wait_send()

        @pl.loop(0, NZ)
        def _(j):
            for p in range(2):
                spread(j, p, i).wait_send()

    @pl.loop(0, NZ)
    def _(j):
        @pl.when((j <= zl) & (zl < NZ - 1))
        def _():
            code_chain(0, j).wait_send()
            for p in range(2):
                chain(0, j, p).wait_send()

        @pl.when((j >= zl) & (zl > 0))
        def _():
            code_chain(1, j).wait_send()
            for p in range(2):
                chain(1, j, p).wait_send()

    for a in range(2):
        for h in range(2):
            z_send(a, h).wait_send()
            for u, base in ((me, 0), (other, 4)):
                for cp in y_send(a, u, h, base):
                    cp.wait_send()
            for n in range(8):
                core_send(a, me, h, n).wait_send()

    for a in range(2):
        zs(a).wait_send()
        for u in range(8):
            cs(a, u).wait_send()
        for i in range(1, 4):
            for h in range(2):
                ys(a, i, h).wait_send()

    @pl.loop(0, NZ)
    def _(j):
        for p in range(2):
            for i in range(1, 4):
                xs(j, p, i).wait_send()

        @pl.when(j < zl)
        def _():
            for p in range(2):
                left(j, p).wait_send()

        @pl.when(j > zl)
        def _():
            for p in range(2):
                right(j, p).wait_send()


def vmem():
    return pl.BlockSpec(memory_space=pltpu.VMEM)


def shards(tokens, w_up, up_feat, up_hid, up_count, w_down, down_feat, down_hid, down_count, grad_out):
    V, S, I32 = pltpu.VMEM, pltpu.SMEM, jnp.int32
    scratch = [
        V((ROWS, 3, BLK, TOK), BF), V((ROWS, 3, BLK, TOK), BF), V((NX, NZ) + WTILE, BF), V((NX, NZ, 1, 128), I32),
        V((TOK, FEAT), BF), V((TOK, FEAT), BF), V((BLK, CAP * BLK), BF), V((BLK, CAP * BLK), BF),
        S((1, CAP), I32), S((1, CAP), I32), S((1, 1), I32), S((1, CAP), I32), S((1, CAP), I32), S((1, 1), I32),
        dma((10,)),
        dma((2, 2, 16)), dma((2, ROWS)), dma((2, NZ, 2)), dma((NZ, 2)), dma((NZ, 4, 2)), dma((NX, NZ, 2)),
        dma((2, NZ)), dma((NZ,)), dma((4,)), dma((4,)),
        S((NX, NZ, 1, 128), I32), V((128, 128), I32), V((8, 128), I32), S((8, 128), I32),
        V((ROWS * CAP, BLK, TOK), F32), V((ROWS * CAP, BLK, TOK), F32), V((ROWS * CAP + 1, BLK, TOK), F32),
        V((HB, BLK, TOK), BF), V((HB, BLK, TOK), F32), V((HB, BLK, TOK), BF),
        V((2, ROWS, HALF, CAP * BLK), BF), V((2, UNITS) + UNIT, BF), V((NX, NZ) + WTILE, BF),
        V((2, 8) + UNIT, BF), V((2, 8) + UNIT, BF), V((2, 3, 2) + UNIT, BF), V((2,) + UNIT, BF), V((2,) + UNIT, BF),
        V((3, NZ) + WTILE, BF), V((NZ,) + WTILE, BF), V((NZ,) + WTILE, BF), V((NZ,) + WTILE, BF),
        V((BLK, CAP * BLK), F32),
        dma((2, 8)), dma((2, 8)), dma((2, 3, 2)), dma((2, 3, 2)), dma((2,)), dma((2,)),
        dma((8, 4, 2)), dma((8, 4, 2)), dma((8, 2)), dma((8, 2)), dma((8, 2)), dma((8, 2)),
    ]
    return pl.pallas_call(
        kernel,
        name="ffn",
        out_shape=(
            jax.ShapeDtypeStruct((TOK, FEAT), BF),
            jax.ShapeDtypeStruct((TOK, FEAT), BF),
            jax.ShapeDtypeStruct((BLK, CAP * BLK), BF),
            jax.ShapeDtypeStruct((BLK, CAP * BLK), BF),
        ),
        in_specs=[pl.BlockSpec(memory_space=pltpu.HBM)] * 10,
        out_specs=(vmem(),) * 4,
        scratch_shapes=scratch,
        compiler_params=pltpu.CompilerParams(
            collective_id=0, has_side_effects=True, vmem_limit_bytes=VMEM_LIMIT
        ),
    )(tokens, grad_out, w_up, w_down, up_feat, up_hid, up_count, down_feat, down_hid, down_count)


def solution(mesh):
    return jax.shard_map(
        shards,
        mesh=mesh,
        in_specs=(P("row", "col"),) * 10,
        out_specs=(P("row", "col"),) * 4,
        check_vma=False,
    )
```

```python
import jax
import jax.numpy as jnp
from jax import lax
from jax.experimental import pallas as pl
from jax.experimental.pallas import tpu as pltpu
from jax.sharding import PartitionSpec as P

BLK = 64
CAP = 4
TOK = 128
FEAT = 384
HALF = 192
HB = 24
NX, NY, NZ = 4, 4, 8
UNITS = 16
ROWS = 32
GELU_SCALE = 0.7978845608028654
GELU_CUBIC = 0.044715
MESH = pl.DeviceIdType.MESH
BF = jnp.bfloat16
F32 = jnp.float32
VMEM_LIMIT = 60 << 20
dma = pltpu.SemaphoreType.DMA
WTILE = (2, BLK, CAP * BLK)
UNIT = (2, HALF, TOK)
UF, UH, DF, DH = 0, 4, 8, 12


def coords():
    row, col = lax.axis_index("row"), lax.axis_index("col")
    return row % 4, col // 4, row // 4, (col // 2) % 2, col % 2


def dev(x, y, zl, zh, c):
    return (zl * 4 + x, y * 4 + zh * 2 + c)


def unit(y, zh, c):
    return y * 4 + zh * 2 + c


def remote(src, dst, ss, rs, to):
    return pltpu.make_async_remote_copy(
        src_ref=src, dst_ref=dst, send_sem=ss, recv_sem=rs, device_id=to, device_id_type=MESH
    )


def hello(x, y, zl, zh, c):
    barrier = pltpu.get_barrier_semaphore()

    def signal(to):
        pl.semaphore_signal(barrier, inc=1, device_id=to, device_id_type=MESH)

    for i in range(1, 4):
        signal(dev((x + i) % 4, y, zl, zh, c))
        signal(dev(x, (y + i) % 4, zl, zh, c))
    signal(dev(x, y, zl, 1 - zh, c))
    signal(dev(x, y, zl, zh, 1 - c))

    signal(dev(x, y, (zl + 1) % 8, jnp.where(zl == NZ - 1, 1 - zh, zh), c))
    signal(dev(x, y, (zl + 7) % 8, jnp.where(zl == 0, 1 - zh, zh), c))


def gelu_parts(v):
    t = jnp.tanh(GELU_SCALE * (v + GELU_CUBIC * v * v * v))
    values = 0.5 * v * (1.0 + t)
    slope = 0.5 * (1.0 + t) + 0.5 * v * (1.0 - t * t) * GELU_SCALE * (1.0 + 3.0 * GELU_CUBIC * v * v)
    return values, slope


def dot(a, b):
    return jnp.dot(a, b, preferred_element_type=F32)


def dot_nt(a, b):
    return lax.dot_general(a, b, (((1,), (1,)), ((), ())), preferred_element_type=F32)


def kernel(
    tok_h, grad_h, wup_h, wdn_h, uf_h, uh_h, uc_h, df_h, dh_h, dc_h,
    mixed, gin, gup, gdn,
    T0, T1, W, C, tok, grad, wup, wdn, uf, uh, uc, df, dh, dc, in_sem,
    t_send, t_recv, wz_send, wz_recv, wx_send, wx_recv, cz_send, cz_recv, cx_send, cx_recv,
    codes, table, order_v, order, p1, p2, run, act, slope, gp,
    M, G, rc, s1, ry, s2, rz, rx, sz, rl, rr, total,
    c_send, c_recv, y_sem_send, y_sem_recv, z_sem_send, z_sem_recv, x_send, x_recv,
    l_send, l_recv, r_send, r_recv,
):
    x, y, zl, zh, c = coords()
    T = (T0, T1)
    me, other = unit(y, zh, c), unit(y, 1 - zh, c)
    hbm = (tok_h, wup_h, wdn_h, uf_h, uh_h, uc_h, df_h, dh_h, dc_h, grad_h)
    local = (tok, wup, wdn, uf, uh, uc, df, dh, dc, grad)
    loads = [pltpu.make_async_copy(p, q, in_sem.at[n]) for n, (p, q) in enumerate(zip(hbm, local))]
    for cp in loads:
        cp.start()
    hello(x, y, zl, zh, c)

    def turn(a, ref):
        T[a][pl.ds(2 * me, 2)] = ref[...].astype(F32).T.astype(BF).reshape(2, 3, BLK, TOK)

    loads[0].wait()
    turn(0, tok)
    for cp in loads[1:9]:
        cp.wait()
    lane = lax.broadcasted_iota(jnp.int32, (1, 128), 1)
    code = jnp.zeros((1, 128), jnp.int32)
    for base, ref in ((0, uf), (4, uh), (8, df), (12, dh)):
        for s in range(CAP):
            code = jnp.where(lane == base + s, ref[0, s], code)
    C[x, zl] = code
    slot = lax.broadcasted_iota(jnp.int32, (BLK, CAP * BLK), 1) // BLK
    zero = jnp.zeros((BLK, CAP * BLK), F32)
    W[x, zl, 0] = jnp.where(slot < uc[0, 0], wup[...].astype(F32), zero).astype(BF)
    W[x, zl, 1] = jnp.where(slot < dc[0, 0], wdn[...].astype(F32), zero).astype(BF)
    loads[9].wait()
    turn(1, grad)
    pl.semaphore_wait(pltpu.get_barrier_semaphore(), 10)

    def chain(way, j, p):
        to = dev(x, y, zl + (1 if way == 0 else -1), zh, c)
        ref = W.at[x, j, p]
        return remote(ref, ref, wz_send.at[way, j, p], wz_recv.at[j, p], to)

    def code_chain(way, j):
        to = dev(x, y, zl + (1 if way == 0 else -1), zh, c)
        return remote(C.at[x, j], C.at[x, j], cz_send.at[way, j], cz_recv.at[j], to)

    def chain_start(way, j, p):
        @pl.when((zl < NZ - 1) if way == 0 else (zl > 0))
        def _():
            chain(way, j, p).start()
            if p == 0:
                code_chain(way, j).start()

    def spread(j, p, i):
        to = dev((x + i) % 4, y, zl, zh, c)
        ref = W.at[x, j, p]
        return remote(ref, ref, wx_send.at[j, i, p], wx_recv.at[x, j, p], to)

    def spread_start(j, p):
        for i in (1, 3, 2):
            spread(j, p, i).start()

    def t_copy(a, u, h, kind, to):
        ref = T[a].at[2 * u + h]
        return remote(ref, ref, t_send.at[a, h, kind], t_recv.at[a, 2 * u + h], to)

    def y_send(a, u, h, base):
        return [
            t_copy(a, u, h, base + n, dev(x, (y + i) % 4, zl, zh, c)) for n, i in enumerate((1, 3, 2))
        ]

    def core_send(a, u, h, n):
        return t_copy(a, u, h, 8 + n, dev(x, y, zl, zh, 1 - c))

    def z_send(a, h):
        return t_copy(a, me, h, 3, dev(x, y, zl, 1 - zh, c))

    def t_wait(a, u, h):
        t_copy(a, u, h, 7, dev(x, y, zl, zh, 1 - c)).wait_recv()

    def own(a):
        for h in range(2):
            for cp in y_send(a, me, h, 0):
                cp.start()
            core_send(a, me, h, 0).start()

    def near(a):
        for h in range(2):
            for n, i in enumerate((1, 3, 2)):
                u = unit((y + i) % 4, zh, c)
                t_wait(a, u, h)
                core_send(a, u, h, 2 + n).start()

    def partner(a, h):
        t_wait(a, other, h)
        for cp in y_send(a, other, h, 4):
            cp.start()
        core_send(a, other, h, 1).start()

    def far(a, h):
        for n, i in enumerate((1, 3, 2)):
            u = unit((y + i) % 4, 1 - zh, c)
            t_wait(a, u, h)
            core_send(a, u, h, 5 + n).start()

    def pull(t):
        for p in range(2):
            @pl.when(zl - t >= 0)
            def _():
                j = zl - t
                chain(0, j, p).wait_recv()
                if p == 0:
                    code_chain(0, j).wait_recv()
                chain_start(0, j, p)
                spread_start(j, p)

            @pl.when(zl + t <= NZ - 1)
            def _():
                j = zl + t
                chain(1, j, p).wait_recv()
                if p == 0:
                    code_chain(1, j).wait_recv()
                chain_start(1, j, p)
                spread_start(j, p)


    def xs(j, p, i):
        xt = (x + i) % 4
        return remote(
            G.at[xt, j, p], rx.at[i - 1, j, p], x_send.at[j, i, p], x_recv.at[j, i, p], dev(xt, y, zl, zh, c)
        )

    def cs(a, u):
        return remote(
            M.at[a, 2 * u + 1 - c], rc.at[a, u], c_send.at[a, u], c_recv.at[a, u], dev(x, y, zl, zh, 1 - c)
        )

    def ys(a, i, h):
        yt = (y + i) % 4
        return remote(
            s1.at[a, yt * 2 + h], ry.at[a, i - 1, h], y_sem_send.at[a, i - 1, h], y_sem_recv.at[a, i - 1, h],
            dev(x, yt, zl, zh, c),
        )

    def zs(a):
        return remote(s2.at[a], rz.at[a], z_sem_send.at[a], z_sem_recv.at[a], dev(x, y, zl, 1 - zh, c))

    def x_unit(j, p):
        for i in (1, 3, 2):
            xs(j, p, i).start()

    def add_core(a, u):
        cs(a, u).wait_recv()
        s1[a, u] = (M[a, 2 * u + c].astype(F32) + rc[a, u].astype(F32)).astype(BF)

    def core_stage(a):
        for h in (0, 1):
            hh = jnp.where(h == 0, 1 - zh, zh)
            for i in (1, 3, 2):
                add_core(a, ((y + i) % 4) * 2 + hh)
                ys(a, i, hh).start()
        for h in range(2):
            add_core(a, y * 2 + h)

    def y_sum(a, h):
        for i in range(1, 4):
            ys(a, i, h).wait_recv()
        acc = s1[a, y * 2 + h].astype(F32)
        for i in range(3):
            acc = acc + ry[a, i, h].astype(F32)
        return acc

    def y_stage(a):
        s2[a] = y_sum(a, 1 - zh).astype(BF)
        zs(a).start()

    def z_stage(a, out):
        own = y_sum(a, zh)
        zs(a).wait_recv()
        out[...] = (own + rz[a].astype(F32)).reshape(FEAT, TOK).T.astype(BF)

    def x_sum(j, p):
        for i in range(1, 4):
            xs(j, p, i).wait_recv()
        acc = G[x, j, p].astype(F32)
        for i in range(3):
            acc = acc + rx[i, j, p].astype(F32)
        return acc

    def left(j, p):
        to = dev(x, y, zl - 1, zh, c)
        return remote(sz.at[j, p], rl.at[j, p], l_send.at[j, p], l_recv.at[j, p], to)

    def right(j, p):
        to = dev(x, y, zl + 1, zh, c)
        return remote(sz.at[j, p], rr.at[j, p], r_send.at[j, p], r_recv.at[j, p], to)

    def pass_on(j, p, move, got, first):
        acc = x_sum(j, p)

        @pl.when(first)
        def _():
            sz[j, p] = acc.astype(BF)

        @pl.when(jnp.logical_not(first))
        def _():
            move(j, p).wait_recv()
            sz[j, p] = (acc + got[j, p].astype(F32)).astype(BF)

        move(j, p).start()

    def step(t, p):
        @pl.when(t >= NZ - 1 - zl)
        def _():
            pass_on(t - NZ + 1 + zl, p, left, rl, zl == NZ - 1)

        @pl.when(t >= zl)
        def _():
            pass_on(NZ - 1 - t + zl, p, right, rr, zl == 0)


    def code(r, k):
        return codes[r % 4, r // 4, 0, k]

    def forward(j, xx):
        r = j * 4 + xx
        wt = W[xx, j, 0].astype(F32).T.astype(BF)
        for s in range(CAP):
            p1[r * CAP + s] = dot(wt[s * BLK : (s + 1) * BLK], T[0][r, code(r, UF + s)])

    def backward(j, xx):
        r = j * 4 + xx
        w = W[xx, j, 1]
        for s in range(CAP):
            p2[r * CAP + s] = dot(w[:, s * BLK : (s + 1) * BLK], T[1][r, code(r, DF + s)])

    def slot_masks(r, base):
        lane = lax.broadcasted_iota(jnp.int32, (1, CAP * BLK), 1) // BLK
        which = jnp.zeros((1, CAP * BLK), jnp.int32)
        for s in range(CAP):
            which = jnp.where(lane == s, code(r, base + s), which)
        return [jnp.where(which == f, 1.0, 0.0).astype(BF) for f in range(3)]

    def mixed_tile(r):
        w = W[r % 4, r // 4, 1].astype(F32)
        w = jnp.concatenate([w[:, s * BLK : (s + 1) * BLK].T for s in range(CAP)], axis=1).astype(BF)
        lhs = jnp.concatenate([w * m for m in slot_masks(r, DF)], axis=0)
        rhs = jnp.concatenate([act[code(r, DH + s)] for s in range(CAP)], axis=0)
        M[0, r // 2, r % 2] = dot(lhs, rhs).astype(BF)

    def input_tile(r):
        w = W[r % 4, r // 4, 0]
        lhs = jnp.concatenate([w * m for m in slot_masks(r, UF)], axis=0)
        rhs = jnp.concatenate([gp[code(r, UH + s)] for s in range(CAP)], axis=0)
        M[1, r // 2, r % 2] = dot(lhs, rhs).astype(BF)

    def down_tile(j, xx):
        r = j * 4 + xx
        parts = [dot_nt(act[code(r, DH + s)], T[1][r, code(r, DF + s)]) for s in range(CAP)]
        G[xx, j, 1] = jnp.concatenate(parts, axis=1).astype(BF)

    def up_tile(j, xx):
        r = j * 4 + xx
        parts = [dot_nt(T[0][r, code(r, UF + s)], gp[code(r, UH + s)]) for s in range(CAP)]
        G[xx, j, 0] = jnp.concatenate(parts, axis=1).astype(BF)

    def sort_slots(base, row):
        col_at = lax.broadcasted_iota(jnp.int32, (ROWS, 1), 0)
        lane128 = lax.broadcasted_iota(jnp.int32, (ROWS, 128), 1)
        keys = table[0:ROWS, :]
        turned = table[...].T
        perm = jnp.zeros((1, 128), jnp.int32)
        sorted_keys = jnp.zeros((1, 128), jnp.int32)
        below = jnp.zeros((1, 128), jnp.int32)
        for s in range(CAP):
            mine = jnp.sum(jnp.where(lane128 == base + s, keys, 0), axis=1, keepdims=True)
            rank = jnp.zeros((ROWS, 1), jnp.int32)
            for o in range(CAP):
                theirs = turned[base + o : base + o + 1, :]
                first = (theirs < mine) | ((theirs == mine) & (o * ROWS + lane128 < s * ROWS + col_at))
                first = first & (lane128 < ROWS)
                rank = rank + jnp.sum(jnp.where(first, 1, 0), axis=1, keepdims=True)
            here = rank == lane128
            perm = perm + jnp.sum(jnp.where(here, col_at * CAP + s, 0), axis=0, keepdims=True)
            sorted_keys = sorted_keys + jnp.sum(jnp.where(here, mine, 0), axis=0, keepdims=True)
            below = below + jnp.sum(jnp.where(mine < lane128, 1, 0), axis=0, keepdims=True)
        order_v[row : row + 1] = perm
        order_v[row + 1 : row + 2] = sorted_keys
        order_v[row + 2 : row + 3] = below

    def segment_sums(src, row):
        def add(i, carry):
            keep = order[row + 1, i] == order[row + 1, jnp.maximum(i - 1, 0)]
            carry = jnp.where(keep, carry, 0.0) + src[order[row, i]]
            run[i + 1] = carry
            return carry

        lax.fori_loop(0, ROWS * CAP, add, jnp.zeros((BLK, TOK), F32), unroll=4)

    def segment(row, k):
        last = order[row + 2, k + 1]
        return jnp.where(last > order[row + 2, k], run[last], 0.0)

    def tiles(fn, start=0, end=NZ):
        @pl.loop(start, end)
        def _(j):
            for xx in range(NX):
                fn(j, xx)

    def units(fn, a, mine):
        @pl.loop(0, 8)
        def _(n):
            v = 2 * (n % 4) + jnp.where(n < 4, 1 - zh, zh)
            u = 2 * v + (c if mine else 1 - c)
            for h in range(2):
                fn(2 * u + h)
            if not mine:
                cs(a, v).start()

    def wave(fn, p):
        def one(j):
            for xx in range(NX):
                fn(j, xx)
            x_unit(j, p)

        @pl.loop(0, NZ - 1)
        def _(t):
            @pl.when(t >= NZ - 1 - zl)
            def _():
                one(t - NZ + 1 + zl)

            @pl.when(t >= zl)
            def _():
                one(NZ - 1 - t + zl)

        one(zl)
    for p in range(2):
        chain_start(0, zl, p)
        chain_start(1, zl, p)
        if p == 0:
            z_send(0, 0).start()
        spread_start(zl, p)
    def code_send(i):
        to = dev((x + i) % 4, y, zl, zh, c)
        return remote(C.at[x], C.at[x], cx_send.at[i], cx_recv.at[x], to)

    def code_sends():
        for i in range(1, 4):
            code_send(i).start()

    to_smem = pltpu.make_async_copy(C, codes, in_sem.at[0])
    order_copy = pltpu.make_async_copy(order_v, order, in_sem.at[1])

    def settle():
        for i in range(1, 4):
            xt = (x + i) % 4
            to = dev(xt, y, zl, zh, c)
            remote(C.at[xt], C.at[xt], cx_send.at[i], cx_recv.at[xt], to).wait_recv()
        to_smem.start()
        table[...] = jnp.zeros_like(table)
        order_v[...] = jnp.zeros_like(order_v)
        run[0] = jnp.zeros((BLK, TOK), F32)
        for r in range(ROWS):
            table[r : r + 1] = C[r % 4, r // 4]
        sort_slots(UH, 0)
        sort_slots(DH, 3)
        order_copy.start()
        for i in range(1, 4):
            xt = (x + i) % 4
            to = dev(xt, y, zl, zh, c)

            @pl.loop(0, NZ)
            def _(j):
                for p in range(2):
                    ref = W.at[xt, j, p]
                    remote(ref, ref, wx_send.at[j, i, p], wx_recv.at[xt, j, p], to).wait_recv()

        to_smem.wait()
        order_copy.wait()

    def core_wait(a):
        @pl.loop(0, 8)
        def _(v):
            for h in range(2):
                t_wait(a, 2 * v + 1 - c, h)

    def gelu():
        @pl.loop(0, HB)
        def _(k):
            v, d = gelu_parts(segment(0, k))
            act[k] = v.astype(BF)
            slope[k] = d

    def grad_pre():
        @pl.loop(0, HB)
        def _(k):
            gp[k] = (segment(3, k) * slope[k]).astype(BF)

    own(0)
    z_send(0, 1).start()
    own(1)
    pull(1)
    pull(2)
    near(0)
    pull(3)
    z_send(1, 0).start()
    partner(0, 0)
    pull(4)
    z_send(1, 1).start()
    partner(0, 1)
    near(1)
    pull(5)
    far(0, 0)
    pull(6)
    far(0, 1)
    partner(1, 0)
    pull(7)
    code_sends()
    partner(1, 1)
    settle()
    core_wait(0)
    tiles(forward)
    far(1, 0)
    far(1, 1)
    segment_sums(p1, 0)
    gelu()
    units(mixed_tile, 0, False)
    core_wait(1)
    wave(down_tile, 1)
    units(mixed_tile, 0, True)
    core_stage(0)
    tiles(backward)
    step(0, 1)
    segment_sums(p2, 3)
    grad_pre()
    step(1, 1)
    wave(up_tile, 0)
    step(0, 0)
    y_stage(0)
    step(2, 1)
    units(input_tile, 1, False)
    step(1, 0)
    step(3, 1)
    units(input_tile, 1, True)
    step(2, 0)
    step(4, 1)
    core_stage(1)
    step(3, 0)
    step(5, 1)
    step(4, 0)
    step(6, 1)
    y_stage(1)
    step(5, 0)
    step(6, 0)
    owns = []
    for p in range(2):
        total[...] = x_sum(zl, p)

        @pl.when(zl < NZ - 1)
        def _():
            left(zl, p).wait_recv()
            total[...] += rl[zl, p].astype(F32)

        @pl.when(zl > 0)
        def _():
            right(zl, p).wait_recv()
            total[...] += rr[zl, p].astype(F32)

        owns.append(total[...])
    slot = lax.broadcasted_iota(jnp.int32, (BLK, CAP * BLK), 1) // BLK
    gup[...] = jnp.where(slot < uc[0, 0], owns[0], 0.0).astype(BF)
    gdn[...] = jnp.where(slot < dc[0, 0], owns[1], 0.0).astype(BF)
    z_stage(0, mixed)
    z_stage(1, gin)

    for i in range(1, 4):
        code_send(i).wait_send()

        @pl.loop(0, NZ)
        def _(j):
            for p in range(2):
                spread(j, p, i).wait_send()

    @pl.loop(0, NZ)
    def _(j):
        @pl.when((j <= zl) & (zl < NZ - 1))
        def _():
            code_chain(0, j).wait_send()
            for p in range(2):
                chain(0, j, p).wait_send()

        @pl.when((j >= zl) & (zl > 0))
        def _():
            code_chain(1, j).wait_send()
            for p in range(2):
                chain(1, j, p).wait_send()

    for a in range(2):
        for h in range(2):
            z_send(a, h).wait_send()
            for u, base in ((me, 0), (other, 4)):
                for cp in y_send(a, u, h, base):
                    cp.wait_send()
            for n in range(8):
                core_send(a, me, h, n).wait_send()

    for a in range(2):
        zs(a).wait_send()
        for u in range(8):
            cs(a, u).wait_send()
        for i in range(1, 4):
            for h in range(2):
                ys(a, i, h).wait_send()

    @pl.loop(0, NZ)
    def _(j):
        for p in range(2):
            for i in range(1, 4):
                xs(j, p, i).wait_send()

        @pl.when(j < zl)
        def _():
            for p in range(2):
                left(j, p).wait_send()

        @pl.when(j > zl)
        def _():
            for p in range(2):
                right(j, p).wait_send()


def vmem():
    return pl.BlockSpec(memory_space=pltpu.VMEM)


def shards(tokens, w_up, up_feat, up_hid, up_count, w_down, down_feat, down_hid, down_count, grad_out):
    V, S, I32 = pltpu.VMEM, pltpu.SMEM, jnp.int32
    scratch = [
        V((ROWS, 3, BLK, TOK), BF), V((ROWS, 3, BLK, TOK), BF), V((NX, NZ) + WTILE, BF), V((NX, NZ, 1, 128), I32),
        V((TOK, FEAT), BF), V((TOK, FEAT), BF), V((BLK, CAP * BLK), BF), V((BLK, CAP * BLK), BF),
        S((1, CAP), I32), S((1, CAP), I32), S((1, 1), I32), S((1, CAP), I32), S((1, CAP), I32), S((1, 1), I32),
        dma((10,)),
        dma((2, 2, 16)), dma((2, ROWS)), dma((2, NZ, 2)), dma((NZ, 2)), dma((NZ, 4, 2)), dma((NX, NZ, 2)),
        dma((2, NZ)), dma((NZ,)), dma((4,)), dma((4,)),
        S((NX, NZ, 1, 128), I32), V((128, 128), I32), V((8, 128), I32), S((8, 128), I32),
        V((ROWS * CAP, BLK, TOK), F32), V((ROWS * CAP, BLK, TOK), F32), V((ROWS * CAP + 1, BLK, TOK), F32),
        V((HB, BLK, TOK), BF), V((HB, BLK, TOK), F32), V((HB, BLK, TOK), BF),
        V((2, UNITS) + UNIT, BF), V((NX, NZ) + WTILE, BF),
        V((2, 8) + UNIT, BF), V((2, 8) + UNIT, BF), V((2, 3, 2) + UNIT, BF), V((2,) + UNIT, BF), V((2,) + UNIT, BF),
        V((3, NZ) + WTILE, BF), V((NZ,) + WTILE, BF), V((NZ,) + WTILE, BF), V((NZ,) + WTILE, BF),
        V((BLK, CAP * BLK), F32),
        dma((2, 8)), dma((2, 8)), dma((2, 3, 2)), dma((2, 3, 2)), dma((2,)), dma((2,)),
        dma((8, 4, 2)), dma((8, 4, 2)), dma((8, 2)), dma((8, 2)), dma((8, 2)), dma((8, 2)),
    ]
    return pl.pallas_call(
        kernel,
        name="ffn",
        out_shape=(
            jax.ShapeDtypeStruct((TOK, FEAT), BF),
            jax.ShapeDtypeStruct((TOK, FEAT), BF),
            jax.ShapeDtypeStruct((BLK, CAP * BLK), BF),
            jax.ShapeDtypeStruct((BLK, CAP * BLK), BF),
        ),
        in_specs=[pl.BlockSpec(memory_space=pltpu.HBM)] * 10,
        out_specs=(vmem(),) * 4,
        scratch_shapes=scratch,
        compiler_params=pltpu.CompilerParams(
            collective_id=0, has_side_effects=True, vmem_limit_bytes=VMEM_LIMIT
        ),
    )(tokens, grad_out, w_up, w_down, up_feat, up_hid, up_count, down_feat, down_hid, down_count)


def solution(mesh):
    return jax.shard_map(
        shards,
        mesh=mesh,
        in_specs=(P("row", "col"),) * 10,
        out_specs=(P("row", "col"),) * 4,
        check_vma=False,
    )
```
